32 devices in a mesh: ctx: 2 (over x), inner: 16 (over z, y, core).
Axes of the slice: x: 2, y: 2, z: 4, core: 2. Of those that a mesh axis runs over, the one named last changes fastest.
Arguments:
- gate_input: float32 [4096, 768], P(('ctx', 'inner')), may hold values from -6 to 6
- value_input: float32 [4096, 768], P(('ctx', 'inner')), may hold values from -6 to 6
- filter_taps: float32 [2048, 768], P('inner'), may hold values from -0.125 to 0.125
- decay_rate: float32 [8, 768], replicated, may hold values from 9.765625e-06 to 0.11, as said below
- mode_coeff: float32 [8, 768], replicated, may hold values from -0.09375 to 0.09375
- boundary_keep: float32 [1, 8, 768], replicated, may hold values from 0.6 to 1
- cotangent: float32 [4096, 768], P(('ctx', 'inner')), may hold values from -6 to 6
Outputs:
- mixed_out: float32 [4096, 768], P(('ctx', 'inner'))
- grad_gate: float32 [4096, 768], P(('ctx', 'inner'))
- grad_value: float32 [4096, 768], P(('ctx', 'inner'))
- grad_filter: float32 [2048, 768], P('inner')
The draws below stay inside these ranges and needn't reach their ends.
Inputs may be any that keep to these rules, and one draw needn't show every extreme that they name: Each decay_rate lies either between 7.6e-07 and 2.3e-05 (a slow mode) or between 0.02 and 0.1 (a fast mode); the mode keeps exp(-decay_rate) of its state a token.
All inputs are finite; a program needn't handle non-finite values.
Results may differ from the reference program's by a relative error of at most 0.00012.
Values sent between devices are 32-bit elements; how exact they have to be, the bound alone decides.
A program may use at most 64 MiB of HBM per device.

```python
import math
import jax
import jax.numpy as jnp
from jax import lax

CHANNELS = 768
MODES = 8
GROUP = 2048
BOUNDARIES = 1
TOKENS = 4096
N_CTX = 2


def draw_decay_rate(key, part):
    key_pick, key_slow, key_fast = jax.random.split(key, 3)
    slow_share = 0.5
    picked = jax.random.bernoulli(key_pick, slow_share, (MODES, CHANNELS))
    slow_rate = jnp.exp(jax.random.uniform(key_slow, (MODES, CHANNELS), jnp.float32, math.log(0.05 / TOKENS), math.log(1.5 / TOKENS)))
    fast_rate = jnp.exp(jax.random.uniform(key_fast, (MODES, CHANNELS), jnp.float32, math.log(0.02), math.log(0.1)))
    return jnp.where(picked, slow_rate, fast_rate).astype(jnp.float32)


def steps_of(own_key, dims, cuts, least, largest):
    def one(dim, shards_of):
        draws = jax.random.uniform(jax.random.fold_in(jax.random.fold_in(own_key, 6), dim), (shards_of,), jnp.float32, least / len(cuts), largest / len(cuts))
        return jnp.repeat(jnp.exp(draws), dims[dim] // shards_of).reshape((-1,) + (1,) * (len(dims) - dim - 1))

    gain = one(*cuts[0])
    for cut in cuts[1:]:
        gain = gain * one(*cut)
    return gain


def scatter_about(stream_key, dims, width, bound, cuts=(), dtype=jnp.bfloat16):
    gain = steps_of(stream_key, dims, cuts, -0.22, 0.18) if cuts else 1.0
    result = jax.random.normal(stream_key, dims, jnp.float32) * width * gain
    return jnp.minimum(jnp.maximum(result, -bound), bound).astype(dtype)


def setup_inputs(seed: int = 0) -> dict:
    key_list = jax.random.split(jax.random.key(seed), 8)
    gate_input = scatter_about(key_list[0], (TOKENS, CHANNELS), 1.0, 6.0, ((0, 32),), jnp.float32)
    value_input = scatter_about(key_list[1], (TOKENS, CHANNELS), 1.0, 6.0, ((0, 32),), jnp.float32)
    filter_taps = scatter_about(key_list[2], (GROUP, CHANNELS), GROUP ** -0.5, 0.125, ((0, 16),), jnp.float32)
    decay_rate = draw_decay_rate(jax.random.fold_in(key_list[7], 71), 0)
    mode_coeff = scatter_about(key_list[4], (MODES, CHANNELS), TOKENS ** -0.5, 0.09375, (), jnp.float32)
    boundary_keep = jnp.clip(jax.random.uniform(key_list[5], (BOUNDARIES, MODES, CHANNELS), jnp.float32, 0.6, 1.0), 0.6, 1.0)
    cotangent = scatter_about(key_list[6], (TOKENS, CHANNELS), 1.0, 6.0, ((0, 32),), jnp.float32)
    return {"gate_input": gate_input, "value_input": value_input, "filter_taps": filter_taps, "decay_rate": decay_rate, "mode_coeff": mode_coeff, "boundary_keep": boundary_keep, "cotangent": cotangent}


def mode_tail(decay_rate, mode_coeff, lag_steps):
    summed_total = jnp.zeros((lag_steps.shape[0], CHANNELS), jnp.float32)
    for mode_index in range(MODES):
        summed_total = summed_total + mode_coeff[mode_index][None, :] * jnp.exp(-decay_rate[mode_index][None, :] * lag_steps[:, None])
    return summed_total

def forward_layer(gate_input, value_input, filter_taps, decay_rate, mode_coeff, boundary_keep):
    lag_steps = jnp.arange(GROUP).astype(jnp.float32)
    kernel = filter_taps + mode_tail(decay_rate, mode_coeff, lag_steps)
    kernel_spec = jnp.fft.rfft(kernel, n=2 * GROUP, axis=0)
    groups = value_input.reshape(N_CTX, GROUP, CHANNELS)

    def conv_group(group_block):
        spec = jnp.fft.rfft(group_block, n=2 * GROUP, axis=0) * kernel_spec
        return jnp.fft.irfft(spec, n=2 * GROUP, axis=0)[:GROUP]
    inside = lax.map(conv_group, groups)
    to_end = GROUP - 1.0 - lag_steps
    group_sums = jnp.stack([jnp.einsum('pc,gpc->gc', jnp.exp(-decay_rate[mode_index][None, :] * to_end[:, None]), groups, precision=lax.Precision.HIGHEST) for mode_index in range(MODES)], 1)
    group_decay = jnp.exp(-decay_rate * GROUP)
    keep_full = jnp.concatenate([boundary_keep, jnp.ones((1, MODES, CHANNELS), jnp.float32)], 0)

    def advance(state, inputs):
        sums_now, keep_now = inputs
        return (keep_now * (group_decay * state + sums_now), state)
    _, starts = lax.scan(advance, jnp.zeros((MODES, CHANNELS), jnp.float32), (group_sums, keep_full))
    from_start = lag_steps + 1.0
    carried = jnp.zeros((N_CTX, GROUP, CHANNELS), jnp.float32)
    for mode_index in range(MODES):
        weight_line = mode_coeff[mode_index][None, :] * jnp.exp(-decay_rate[mode_index][None, :] * from_start[:, None])
        carried = carried + weight_line[None] * starts[:, mode_index][:, None, :]
    mixture = (inside + carried).reshape(TOKENS, CHANNELS)
    return gate_input * mixture

def reference(gate_input, value_input, filter_taps, decay_rate, mode_coeff, boundary_keep, cotangent):

    def layer_only(gate_arg, value_arg, taps_arg):
        return forward_layer(gate_arg, value_arg, taps_arg, decay_rate, mode_coeff, boundary_keep)
    mixed_out, pullback = jax.vjp(layer_only, gate_input, value_input, filter_taps)
    grad_gate, grad_value, grad_filter = pullback(cotangent)
    return (mixed_out, grad_gate, grad_value, grad_filter * TOKENS ** (-0.5))
```

```python
import functools
import math

import jax
import jax.numpy as jnp
import numpy as np
from jax import lax
from jax.experimental import pallas as pl
from jax.experimental.pallas import tpu as pltpu
from jax.sharding import PartitionSpec as P

FULL_PRECISION = lax.Precision.HIGHEST


def prefix(part, axis, combine, identity, reverse):
    count = lax.axis_size(axis)
    place = lax.axis_index(axis)
    ahead = count - 1 - place if reverse else place
    gathered = jax.tree.map(lambda a: lax.all_gather(a, axis), part)
    state = jax.tree.map(lambda a, e: jnp.zeros_like(a) + jnp.asarray(e, a.dtype), part, identity)

    def one(hop, state):
        source = count - 1 - hop if reverse else hop
        return combine(
            state, jax.tree.map(lambda a: lax.dynamic_index_in_dim(a, source, 0, False), gathered)
        )

    return lax.fori_loop(0, ahead, one, state)


def turn_table(left_index, right_index, period):
    phase = (left_index * right_index % period).astype(jnp.float32) * (2.0 * math.pi / period)
    return (jnp.cos(phase), jnp.sin(phase))


def ahead_table(cosine, sine):
    return jnp.stack([jnp.stack([cosine, sine], 0), jnp.stack([-sine, cosine], 0)], 0)


def behind_table(cosine, sine):
    return jnp.stack([jnp.stack([cosine, -sine], 0), jnp.stack([sine, cosine], 0)], 0)


def contract(form, table, data):
    return jnp.einsum(form, table, data, precision=FULL_PRECISION)


def combine_links(earlier, later_link):
    return (later_link[0] * earlier[0], later_link[0] * earlier[1] + later_link[1])


def carried_mode_state(decay_factors, partial_terms, backward_pass):
    unit_links = jnp.ones_like(decay_factors)
    blank_terms = jnp.zeros_like(partial_terms)
    summed_total = lax.psum(partial_terms, "inner")
    return prefix(
        (decay_factors, summed_total),
        "ctx",
        combine_links,
        (unit_links, blank_terms),
        backward_pass,
    )[1]


def shards(gate_input, value_input, filter_taps, decay_rate, mode_coeff, boundary_keep, cotangent):
    tok_dev = value_input.shape[0]
    inner_count = lax.axis_size("inner")
    ctx_count = lax.axis_size("ctx")
    group_len = tok_dev * inner_count
    fft_len = 2 * group_len
    row_count = 2 * inner_count
    col_count = tok_dev // inner_count
    inner_idx = lax.axis_index("inner")
    ctx_idx = lax.axis_index("ctx")
    row_range = jnp.arange(row_count, dtype=jnp.int32)
    inner_range = jnp.arange(inner_count, dtype=jnp.int32)
    tok_range = jnp.arange(tok_dev, dtype=jnp.int32)
    owner_of_row = row_range // 2
    mirrored_label = jnp.where(owner_of_row == 0, inner_count, row_count - owner_of_row)
    row_label = jnp.where(row_range % 2 == 0, owner_of_row, mirrored_label)
    cos_rows, sin_rows = turn_table(row_label[:, None], inner_range[None, :], row_count)
    rows_table = ahead_table(cos_rows, sin_rows)
    col_index = inner_idx * col_count + jnp.arange(col_count, dtype=jnp.int32)
    cos_twist, sin_twist = turn_table(row_label[:, None, None], col_index[None, :, None], fft_len)
    cos_line, sin_line = turn_table(tok_range[:, None], tok_range[None, :], tok_dev)
    line_ahead = ahead_table(cos_line, sin_line)
    line_behind = behind_table(cos_line, sin_line)
    own_rows = lax.dynamic_slice_in_dim(row_label, 2 * inner_idx, 2, 0)
    cos_untwist, sin_untwist = turn_table(
        own_rows[:, None, None], tok_range[None, :, None], fft_len
    )
    cos_back, sine_reverse = turn_table(inner_range[:, None], row_label[None, :], row_count)
    back_table = behind_table(cos_back, sine_reverse)

    def to_spectrum(signals):
        stacked = jnp.stack(signals, 0)[:, None]
        columns = lax.all_to_all(stacked, "inner", split_axis=2, concat_axis=1, tiled=True)
        count = len(signals)
        parts = contract("pqki,qijc->pkjc", rows_table[:, :count], columns)
        turned = jnp.stack(
            [
                parts[0] * cos_twist + parts[1] * sin_twist,
                parts[1] * cos_twist - parts[0] * sin_twist,
            ],
            0,
        )
        spread = lax.all_to_all(turned, "inner", split_axis=1, concat_axis=2, tiled=True)
        return contract("pqkj,qbjc->pbkc", line_ahead, spread)

    def from_spectrum(spec, keep_imag):
        line = contract("pqjk,qbkc->pbjc", line_behind, spec)
        turned = jnp.stack(
            [
                line[0] * cos_untwist - line[1] * sin_untwist,
                line[1] * cos_untwist + line[0] * sin_untwist,
            ],
            0,
        )
        back = lax.all_to_all(turned, "inner", split_axis=2, concat_axis=1, tiled=True)
        count = 2 if keep_imag else 1
        row_values = contract("pqik,qkjc->pijc", back_table[:count], back) * (1.0 / fft_len)
        joined = lax.all_to_all(row_values, "inner", split_axis=1, concat_axis=2, tiled=True)
        return joined[:, 0]

    def mirror_rows(spec):
        flipped = spec[:, ::-1]
        rolled = jnp.roll(flipped, 1, axis=1)
        leading_device = jnp.stack([rolled[0], flipped[1]], 0)
        return jnp.where(inner_idx == 0, leading_device, flipped[::-1])

    def times_kernel_conj(kern, spec):
        return jnp.stack(
            [kern[0] * spec[0] + kern[1] * spec[1], kern[0] * spec[1] - kern[1] * spec[0]], 0
        )

    positions = (inner_idx * tok_dev + tok_range).astype(jnp.float32)
    rate_wide = decay_rate[:, None, :]
    coeff_wide = mode_coeff[:, None, :]
    to_end_pow = jnp.exp(-rate_wide * (group_len - 1.0 - positions)[None, :, None])
    from_start_pow = coeff_wide * jnp.exp(-rate_wide * (positions + 1.0)[None, :, None])
    tail_part = jnp.sum(coeff_wide * jnp.exp(-rate_wide * positions[None, :, None]), 0)
    group_decay = jnp.exp(-decay_rate * float(group_len))
    keep_full = jnp.concatenate(
        [boundary_keep, jnp.ones((1,) + boundary_keep.shape[1:], jnp.float32)], 0
    )
    keep_row = lax.dynamic_index_in_dim(keep_full, ctx_idx, 0, keepdims=False)
    link_decay = keep_row * group_decay
    kernel = filter_taps + tail_part
    kern_spec = to_spectrum((kernel,))
    mix_grad = cotangent * gate_input
    packed = to_spectrum((value_input, mix_grad))
    mirror_real = mirror_rows(packed[0])
    mirror_imag = mirror_rows(packed[1])
    val_spec = jnp.stack([0.5 * (packed[0] + mirror_real), 0.5 * (packed[1] - mirror_imag)], 0)
    grad_spec = jnp.stack([0.5 * (packed[1] + mirror_imag), 0.5 * (mirror_real - packed[0])], 0)
    ahead = jnp.stack(
        [
            kern_spec[0] * val_spec[0] - kern_spec[1] * val_spec[1],
            kern_spec[0] * val_spec[1] + kern_spec[1] * val_spec[0],
        ],
        0,
    )
    behind = times_kernel_conj(kern_spec, grad_spec)
    both_parts = from_spectrum(jnp.stack([ahead[0] - behind[1], ahead[1] + behind[0]], 0), True)
    inside = both_parts[0]
    through = both_parts[1]
    local_sums = jnp.sum(to_end_pow * value_input[None], 1)
    starts = carried_mode_state(link_decay, keep_row * local_sums, False)
    mixture = inside + jnp.sum(from_start_pow * starts[:, None, :], 0)
    mixed_out = gate_input * mixture
    grad_gate = cotangent * mixture
    pull_terms = jnp.sum(from_start_pow * mix_grad[None], 1)
    later_state = carried_mode_state(link_decay, pull_terms, True)
    grad_value = through + jnp.sum(to_end_pow * (keep_row * later_state)[:, None, :], 0)
    corr = times_kernel_conj(val_spec, grad_spec)
    share_spec = lax.psum_scatter(corr, "ctx", scatter_dimension=3, tiled=True)
    share_grad = from_spectrum(share_spec, False)[0]
    grad_filter = lax.all_gather(share_grad, "ctx", axis=1, tiled=True)
    grad_scale = 1.0 / math.sqrt(group_len * ctx_count)
    return (mixed_out, grad_gate, grad_value, grad_filter * grad_scale)


LANES = 128
SUBLANES = 8


def plus(x, y):
    return tuple(q if p is None else p if q is None else p + q for p, q in zip(x, y))


def minus(x, y):
    return tuple(
        p if q is None else -q if p is None else p - q for p, q in zip(x, y)
    )


def scaled(part, factor):
    if part is None or abs(factor) < 1e-12:
        return None
    if abs(factor - 1.0) < 1e-12:
        return part
    if abs(factor + 1.0) < 1e-12:
        return -part
    return part * factor


def turned(x, angle):
    c, s = math.cos(angle), math.sin(angle)
    real = minus((scaled(x[0], c),), (scaled(x[1], s),))[0] if x[1] is not None else scaled(x[0], c)
    imag = plus((scaled(x[0], s),), (scaled(x[1], c),))[0]
    return (real, imag)


def transform_ahead(xs):
    n = len(xs)
    if n == 1:
        return xs
    h = n // 2
    total = [plus(xs[i], xs[i + h]) for i in range(h)]
    apart = [turned(minus(xs[i], xs[i + h]), -2.0 * math.pi * i / n) for i in range(h)]
    even, odd = transform_ahead(total), transform_ahead(apart)
    return [(even, odd)[k % 2][k // 2] for k in range(n)]


def transform_behind(xs):
    n = len(xs)
    if n == 1:
        return xs
    h = n // 2
    even, odd = transform_behind(xs[0::2]), transform_behind(xs[1::2])
    odd = [turned(odd[i], 2.0 * math.pi * i / n) for i in range(h)]
    return [plus(even[i], odd[i]) for i in range(h)] + [minus(even[i], odd[i]) for i in range(h)]


def split_table(table):
    high = table.astype(jnp.bfloat16)
    return high, (table - high.astype(np.float32)).astype(jnp.bfloat16)


def line_tables(width, row_count, half):
    turn = 2.0 * np.pi / width * (np.outer(np.arange(width), np.arange(width)) % width)
    c, s = np.cos(turn), np.sin(turn)
    ahead = np.block([[c, -s], [s, c]]).astype(np.float32)
    behind = np.block([[c, s], [-s, c]]).astype(np.float32)
    length = width * row_count
    phase = 2.0 * np.pi / length * np.outer(np.arange(half), np.arange(width))
    weight = np.full((half, 1), 2.0)
    weight[0] = weight[-1] = 1.0
    twist = np.stack(
        [np.cos(phase), np.sin(phase), np.cos(phase) * weight / length, np.sin(phase) * weight / length]
    ).astype(np.float32)
    return split_table(ahead) + split_table(behind) + (twist,)


def mixer_kernel(
    ctx_count,
    inner_count,
    modes,
    gate,
    value,
    taps,
    rate,
    coeff,
    keep,
    cot,
    ahead_high,
    ahead_low,
    behind_high,
    behind_low,
    twist,
    mixed_out,
    grad_gate,
    grad_value,
    grad_filter,
    send_taps,
    send_value,
    send_grad,
    got_taps,
    got_value,
    got_grad,
    spec,
    params,
    out_mix,
    out_through,
    out_corr,
    back_mix,
    back_through,
    back_corr,
    send_sems,
    recv_sems,
):
    n = ctx_count * inner_count
    width = value.shape[0]
    chans = send_value.shape[1]
    chunks = chans // SUBLANES
    row_count = 2 * inner_count
    half = inner_count + 1
    group_len = width * inner_count
    ctx_idx = lax.axis_index("ctx")
    inner_idx = lax.axis_index("inner")
    me = ctx_idx * inner_count + inner_idx

    barrier = pltpu.get_barrier_semaphore()

    def greet(k, carry):
        d = lax.rem(me + k, n)
        pl.semaphore_signal(
            barrier,
            inc=1,
            device_id=(lax.div(d, inner_count), lax.rem(d, inner_count)),
            device_id_type=pl.DeviceIdType.MESH,
        )
        return carry

    lax.fori_loop(1, n, greet, 0)

    def copy_to(src, dst, kind, d, source):
        return pltpu.make_async_remote_copy(
            src_ref=src,
            dst_ref=dst,
            send_sem=send_sems.at[kind, d],
            recv_sem=recv_sems.at[kind, source],
            device_id=(lax.div(d, inner_count), lax.rem(d, inner_count)),
            device_id_type=pl.DeviceIdType.MESH,
        )

    def everyone(src, dst, kind, fold=False):
        def piece(k, landing):
            d = lax.rem(me + k, n)
            row = lax.rem(d, inner_count) if fold else d
            return copy_to(src.at[row], dst.at[landing], kind, d, landing)

        def start(k, carry):
            piece(k, me).start()
            return carry

        def arrive(k, carry):
            piece(k, lax.rem(me + n - k, n)).wait_recv()
            return carry

        def leave(k, carry):
            piece(k, me).wait_send()
            return carry

        return tuple(
            functools.partial(lax.fori_loop, 1, n, step, 0) for step in (start, arrive, leave)
        )

    def own_group(src, dst, kind):
        def piece(k, landing):
            d = ctx_idx * inner_count + lax.rem(inner_idx + k, inner_count)
            return copy_to(src.at[d], dst.at[landing], kind, d, landing)

        def start(k, carry):
            piece(k, inner_idx).start()
            return carry

        def arrive(k, carry):
            piece(k, lax.rem(inner_idx + inner_count - k, inner_count)).wait_recv()
            return carry

        def leave(k, carry):
            piece(k, inner_idx).wait_send()
            return carry

        return tuple(
            functools.partial(lax.fori_loop, 1, inner_count, step, 0)
            for step in (start, arrive, leave)
        )

    taps_start, taps_arrive, taps_leave = own_group(send_taps, got_taps, 0)
    value_start, value_arrive, value_leave = everyone(send_value, got_value, 1)
    grad_start, grad_arrive, grad_leave = everyone(send_grad, got_grad, 2)
    corr_start, corr_arrive, corr_leave = everyone(out_corr, back_corr, 3, True)
    mix_start, mix_arrive, mix_leave = everyone(out_mix, back_mix, 4)
    through_start, through_arrive, through_leave = everyone(out_through, back_through, 5)

    def by_channel(block):
        return jnp.transpose(block).reshape(n, chans, width)

    send_taps[...] = by_channel(taps[...])
    pl.semaphore_wait(barrier, n - 1)
    taps_start()
    got_taps[inner_idx] = send_taps[me]
    send_value[...] = by_channel(value[...])
    value_start()
    got_value[me] = send_value[me]
    send_grad[...] = by_channel(cot[...] * gate[...])
    grad_start()
    got_grad[me] = send_grad[me]

    rows = [rate[...], coeff[...], keep[...]]
    filled = sum(r.shape[0] for r in rows)
    rows.append(jnp.zeros((LANES - filled, rate.shape[1]), jnp.float32))
    params[...] = jnp.transpose(jnp.concatenate(rows, 0))
    spec[:, half] = jnp.zeros(spec.shape[:1] + spec.shape[2:], jnp.float32)

    lane = lax.broadcasted_iota(jnp.int32, (SUBLANES, width), 1).astype(jnp.float32)

    def per_channel(chunk):
        own = params[pl.ds(pl.multiple_of(me * chans + chunk * SUBLANES, SUBLANES), SUBLANES), :]

        def wide(column):
            return jnp.broadcast_to(own[:, column : column + 1], (SUBLANES, width))

        rates = [wide(m) for m in range(modes)]
        coeffs = [wide(modes + m) for m in range(modes)]
        keeps = [
            [wide((2 + g) * modes + m) for m in range(modes)] for g in range(ctx_count - 1)
        ]
        return rates, coeffs, keeps

    def rows_of(chunk):
        return pl.ds(pl.multiple_of(chunk * SUBLANES, SUBLANES), SUBLANES)

    def add_tail(chunk, carry):
        rates, coeffs, _ = per_channel(chunk)
        steps = [jnp.exp(-r * float(width)) for r in rates]
        terms = [c * jnp.exp(-r * lane) for r, c in zip(rates, coeffs)]
        at = rows_of(chunk)
        for i in range(inner_count):
            got_taps[i, at, :] = got_taps[i, at, :] + sum(terms[1:], terms[0])
            terms = [t * s for t, s in zip(terms, steps)]
        return carry

    def rows_ahead(src, base, slot, chunk):
        at = rows_of(chunk)
        blank = (None, None)
        xs = [(src[base + i, at, :], None) for i in range(inner_count)] + [blank] * inner_count
        parts = transform_ahead(xs)
        for k in range(half):
            real, imag = parts[k]
            c, s = twist[0, k : k + 1, :], twist[1, k : k + 1, :]
            if imag is None:
                first, second = real * c, -(real * s)
            else:
                first, second = real * c + imag * s, imag * c - real * s
            spec[slot, k, at, :width] = first
            spec[slot, k, at, width:] = second

    def line(slot, high, low):
        data = spec[slot].reshape((half + 1) * chans, 2 * width)
        top = data.astype(jnp.bfloat16)
        rest = (data - top.astype(jnp.float32)).astype(jnp.bfloat16)
        dot = functools.partial(jnp.dot, preferred_element_type=jnp.float32)
        result = dot(rest, high[...]) + dot(top, low[...]) + dot(top, high[...])
        spec[slot] = result.reshape(half + 1, chans, 2 * width)

    def rows_behind(slot, chunk):
        at = rows_of(chunk)
        xs = []
        for k in range(half):
            real, imag = spec[slot, k, at, :width], spec[slot, k, at, width:]
            c, s = twist[2, k : k + 1, :], twist[3, k : k + 1, :]
            xs.append((real * c - imag * s, real * s + imag * c))
        xs += [(None, None)] * (row_count - half)
        return [y[0] for y in transform_behind(xs)[:inner_count]]

    def to_spectra(src, first_slot, groups):
        def one(step, carry):
            g = lax.div(step, chunks)
            rows_ahead(src, g * inner_count, first_slot + g, lax.rem(step, chunks))
            return carry

        lax.fori_loop(0, groups * chunks, one, 0)

        def transform(g, carry):
            line(first_slot + g, ahead_high, ahead_low)
            return carry

        lax.fori_loop(0, groups, transform, 0)

    taps_arrive()
    lax.fori_loop(0, chunks, add_tail, 0)
    kern_slot, value_slot, grad_slot = 0, 1, 1 + ctx_count
    to_spectra(got_taps, kern_slot, 1)
    value_arrive()
    to_spectra(got_value, value_slot, ctx_count)
    grad_arrive()
    to_spectra(got_grad, grad_slot, ctx_count)

    def multiply(step, carry):
        k = lax.div(step, chunks)
        at = rows_of(lax.rem(step, chunks))

        def load(slot):
            return spec[slot, k, at, :width], spec[slot, k, at, width:]

        def store(slot, real, imag):
            spec[slot, k, at, :width] = real
            spec[slot, k, at, width:] = imag

        kr, ki = load(kern_slot)
        corr_r = corr_i = 0.0
        for g in range(ctx_count):
            vr, vi = load(value_slot + g)
            gr, gi = load(grad_slot + g)
            corr_r = corr_r + (vr * gr + vi * gi)
            corr_i = corr_i + (vr * gi - vi * gr)
            store(value_slot + g, kr * vr - ki * vi, kr * vi + ki * vr)
            store(grad_slot + g, kr * gr + ki * gi, kr * gi - ki * gr)
        store(kern_slot, corr_r, corr_i)
        return carry

    lax.fori_loop(0, half * chunks, multiply, 0)

    grad_scale = 1.0 / math.sqrt(group_len * ctx_count)
    line(kern_slot, behind_high, behind_low)

    def corr_rows(chunk, carry):
        for i, y in enumerate(rows_behind(kern_slot, chunk)):
            out_corr[i, rows_of(chunk), :] = y * grad_scale
        return carry

    lax.fori_loop(0, chunks, corr_rows, 0)
    corr_start()
    back_corr[me] = out_corr[inner_idx]

    def from_spectra(first_slot, dst):
        def transform(g, carry):
            line(first_slot + g, behind_high, behind_low)
            return carry

        lax.fori_loop(0, ctx_count, transform, 0)

        def one(step, carry):
            g, chunk = lax.div(step, chunks), lax.rem(step, chunks)
            for i, y in enumerate(rows_behind(first_slot + g, chunk)):
                dst[g * inner_count + i, rows_of(chunk), :] = y
            return carry

        lax.fori_loop(0, ctx_count * chunks, one, 0)

    def carried_ahead(chunk, carry):
        rates, coeffs, keeps = per_channel(chunk)
        at = rows_of(chunk)
        steps = [jnp.exp(-r * float(width)) for r in rates]
        whole = [jnp.exp(-r * float(group_len)) for r in rates]
        to_end = [jnp.exp(-r * (width - 1.0 - lane)) for r in rates]
        from_start = [c * jnp.exp(-r * (lane + 1.0)) for r, c in zip(rates, coeffs)]
        state = [jnp.zeros((SUBLANES, 1), jnp.float32)] * modes
        for g in range(ctx_count - 1):
            acc = [jnp.zeros((SUBLANES, width), jnp.float32)] * modes
            for i in range(inner_count):
                block = got_value[g * inner_count + i, at, :]
                acc = [a * s + block for a, s in zip(acc, steps)]
            for m in range(modes):
                total = jnp.sum(acc[m] * to_end[m], 1, keepdims=True)
                state[m] = keeps[g][m][:, :1] * (whole[m][:, :1] * state[m] + total)
            terms = [f * st for f, st in zip(from_start, state)]
            for i in range(inner_count):
                row = (g + 1) * inner_count + i
                out_mix[row, at, :] = out_mix[row, at, :] + sum(terms[1:], terms[0])
                terms = [t * s for t, s in zip(terms, steps)]
        return carry

    def carried_behind(chunk, carry):
        rates, coeffs, keeps = per_channel(chunk)
        at = rows_of(chunk)
        steps = [jnp.exp(-r * float(width)) for r in rates]
        whole = [jnp.exp(-r * float(group_len)) for r in rates]
        to_end = [jnp.exp(-r * (width - 1.0 - lane)) for r in rates]
        from_start = [c * jnp.exp(-r * (lane + 1.0)) for r, c in zip(rates, coeffs)]
        state = [jnp.zeros((SUBLANES, 1), jnp.float32)] * modes
        for g in reversed(range(1, ctx_count)):
            acc = [jnp.zeros((SUBLANES, width), jnp.float32)] * modes
            for i in reversed(range(inner_count)):
                block = got_grad[g * inner_count + i, at, :]
                acc = [a * s + block for a, s in zip(acc, steps)]
            for m in range(modes):
                total = jnp.sum(acc[m] * from_start[m], 1, keepdims=True)
                if g < ctx_count - 1:
                    state[m] = total + whole[m][:, :1] * keeps[g][m][:, :1] * state[m]
                else:
                    state[m] = total
            terms = [
                t * (kp[:, :1] * st) for t, kp, st in zip(to_end, keeps[g - 1], state)
            ]
            for i in reversed(range(inner_count)):
                row = (g - 1) * inner_count + i
                out_through[row, at, :] = out_through[row, at, :] + sum(terms[1:], terms[0])
                terms = [t * s for t, s in zip(terms, steps)]
        return carry

    from_spectra(value_slot, out_mix)
    lax.fori_loop(0, chunks, carried_ahead, 0)
    mix_start()
    back_mix[me] = out_mix[me]
    from_spectra(grad_slot, out_through)
    lax.fori_loop(0, chunks, carried_behind, 0)
    through_start()
    back_through[me] = out_through[me]

    def by_token(blocks):
        return jnp.transpose(blocks[...].reshape(n * chans, width))

    corr_arrive()
    grad_filter[...] = by_token(back_corr)
    mix_arrive()
    mixture = by_token(back_mix)
    mixed_out[...] = gate[...] * mixture
    grad_gate[...] = cot[...] * mixture
    through_arrive()
    grad_value[...] = by_token(back_through)
    for leave in (taps_leave, value_leave, grad_leave, corr_leave, mix_leave, through_leave):
        leave()


def fits(mesh, value_input):
    inner_count, ctx_count = mesh.shape["inner"], mesh.shape["ctx"]
    tok_dev, channels = value_input.shape
    return (
        tok_dev == LANES
        and channels % (inner_count * ctx_count * SUBLANES) == 0
        and inner_count & (inner_count - 1) == 0
    )


def shards_by_channel(
    mesh, gate_input, value_input, filter_taps, decay_rate, mode_coeff, boundary_keep, cotangent
):
    inner_count, ctx_count = mesh.shape["inner"], mesh.shape["ctx"]
    n = inner_count * ctx_count
    tok_dev, channels = value_input.shape
    modes = decay_rate.shape[0]
    chans = channels // n
    half = inner_count + 1
    tables = line_tables(tok_dev, 2 * inner_count, half)
    keep_rows = boundary_keep.reshape(-1, channels)
    block = jax.ShapeDtypeStruct((tok_dev, channels), jnp.float32)
    f32 = functools.partial(pltpu.VMEM, dtype=jnp.float32)
    pieces, own_pieces = f32((n, chans, tok_dev)), f32((inner_count, chans, tok_dev))
    vmem = pl.BlockSpec(memory_space=pltpu.VMEM)
    return pl.pallas_call(
        functools.partial(mixer_kernel, ctx_count, inner_count, modes),
        out_shape=(block,) * 4,
        in_specs=[vmem] * 12,
        out_specs=(vmem,) * 4,
        scratch_shapes=[
            pieces,
            pieces,
            pieces,
            own_pieces,
            pieces,
            pieces,
            f32((1 + 2 * ctx_count, half + 1, chans, 2 * tok_dev)),
            f32((channels, LANES)),
            pieces,
            pieces,
            own_pieces,
            pieces,
            pieces,
            pieces,
            pltpu.SemaphoreType.DMA((6, n)),
            pltpu.SemaphoreType.DMA((6, n)),
        ],
        compiler_params=pltpu.CompilerParams(
            collective_id=0, has_side_effects=True, vmem_limit_bytes=40 * 1024 * 1024
        ),
    )(
        gate_input,
        value_input,
        filter_taps,
        decay_rate,
        mode_coeff,
        keep_rows,
        cotangent,
        *tables,
    )


def shards_of(mesh, *args):
    if fits(mesh, args[1]):
        return shards_by_channel(mesh, *args)
    return shards(*args)


def solution(mesh):
    placed = (
        P(("ctx", "inner"), None),
        P(("ctx", "inner"), None),
        P("inner", None),
        P(),
        P(),
        P(),
        P(("ctx", "inner"), None),
    )
    return jax.shard_map(
        functools.partial(shards_of, mesh),
        mesh=mesh,
        in_specs=placed,
        out_specs=(
            P(("ctx", "inner"), None),
            P(("ctx", "inner"), None),
            P(("ctx", "inner"), None),
            P("inner", None),
        ),
        check_vma=False,
    )
```

```python
import functools
import math

import jax
import jax.numpy as jnp
import numpy as np
from jax import lax
from jax.experimental import pallas as pl
from jax.experimental.pallas import tpu as pltpu
from jax.sharding import PartitionSpec as P

FULL_PRECISION = lax.Precision.HIGHEST


def prefix(part, axis, combine, identity, reverse):
    count = lax.axis_size(axis)
    place = lax.axis_index(axis)
    ahead = count - 1 - place if reverse else place
    gathered = jax.tree.map(lambda a: lax.all_gather(a, axis), part)
    state = jax.tree.map(lambda a, e: jnp.zeros_like(a) + jnp.asarray(e, a.dtype), part, identity)

    def one(hop, state):
        source = count - 1 - hop if reverse else hop
        return combine(
            state, jax.tree.map(lambda a: lax.dynamic_index_in_dim(a, source, 0, False), gathered)
        )

    return lax.fori_loop(0, ahead, one, state)


def turn_table(left_index, right_index, period):
    phase = (left_index * right_index % period).astype(jnp.float32) * (2.0 * math.pi / period)
    return (jnp.cos(phase), jnp.sin(phase))


def ahead_table(cosine, sine):
    return jnp.stack([jnp.stack([cosine, sine], 0), jnp.stack([-sine, cosine], 0)], 0)


def behind_table(cosine, sine):
    return jnp.stack([jnp.stack([cosine, -sine], 0), jnp.stack([sine, cosine], 0)], 0)


def contract(form, table, data):
    return jnp.einsum(form, table, data, precision=FULL_PRECISION)


def combine_links(earlier, later_link):
    return (later_link[0] * earlier[0], later_link[0] * earlier[1] + later_link[1])


def carried_mode_state(decay_factors, partial_terms, backward_pass):
    unit_links = jnp.ones_like(decay_factors)
    blank_terms = jnp.zeros_like(partial_terms)
    summed_total = lax.psum(partial_terms, "inner")
    return prefix(
        (decay_factors, summed_total),
        "ctx",
        combine_links,
        (unit_links, blank_terms),
        backward_pass,
    )[1]


def shards(gate_input, value_input, filter_taps, decay_rate, mode_coeff, boundary_keep, cotangent):
    tok_dev = value_input.shape[0]
    inner_count = lax.axis_size("inner")
    ctx_count = lax.axis_size("ctx")
    group_len = tok_dev * inner_count
    fft_len = 2 * group_len
    row_count = 2 * inner_count
    col_count = tok_dev // inner_count
    inner_idx = lax.axis_index("inner")
    ctx_idx = lax.axis_index("ctx")
    row_range = jnp.arange(row_count, dtype=jnp.int32)
    inner_range = jnp.arange(inner_count, dtype=jnp.int32)
    tok_range = jnp.arange(tok_dev, dtype=jnp.int32)
    owner_of_row = row_range // 2
    mirrored_label = jnp.where(owner_of_row == 0, inner_count, row_count - owner_of_row)
    row_label = jnp.where(row_range % 2 == 0, owner_of_row, mirrored_label)
    cos_rows, sin_rows = turn_table(row_label[:, None], inner_range[None, :], row_count)
    rows_table = ahead_table(cos_rows, sin_rows)
    col_index = inner_idx * col_count + jnp.arange(col_count, dtype=jnp.int32)
    cos_twist, sin_twist = turn_table(row_label[:, None, None], col_index[None, :, None], fft_len)
    cos_line, sin_line = turn_table(tok_range[:, None], tok_range[None, :], tok_dev)
    line_ahead = ahead_table(cos_line, sin_line)
    line_behind = behind_table(cos_line, sin_line)
    own_rows = lax.dynamic_slice_in_dim(row_label, 2 * inner_idx, 2, 0)
    cos_untwist, sin_untwist = turn_table(
        own_rows[:, None, None], tok_range[None, :, None], fft_len
    )
    cos_back, sine_reverse = turn_table(inner_range[:, None], row_label[None, :], row_count)
    back_table = behind_table(cos_back, sine_reverse)

    def to_spectrum(signals):
        stacked = jnp.stack(signals, 0)[:, None]
        columns = lax.all_to_all(stacked, "inner", split_axis=2, concat_axis=1, tiled=True)
        count = len(signals)
        parts = contract("pqki,qijc->pkjc", rows_table[:, :count], columns)
        turned = jnp.stack(
            [
                parts[0] * cos_twist + parts[1] * sin_twist,
                parts[1] * cos_twist - parts[0] * sin_twist,
            ],
            0,
        )
        spread = lax.all_to_all(turned, "inner", split_axis=1, concat_axis=2, tiled=True)
        return contract("pqkj,qbjc->pbkc", line_ahead, spread)

    def from_spectrum(spec, keep_imag):
        line = contract("pqjk,qbkc->pbjc", line_behind, spec)
        turned = jnp.stack(
            [
                line[0] * cos_untwist - line[1] * sin_untwist,
                line[1] * cos_untwist + line[0] * sin_untwist,
            ],
            0,
        )
        back = lax.all_to_all(turned, "inner", split_axis=2, concat_axis=1, tiled=True)
        count = 2 if keep_imag else 1
        row_values = contract("pqik,qkjc->pijc", back_table[:count], back) * (1.0 / fft_len)
        joined = lax.all_to_all(row_values, "inner", split_axis=1, concat_axis=2, tiled=True)
        return joined[:, 0]

    def mirror_rows(spec):
        flipped = spec[:, ::-1]
        rolled = jnp.roll(flipped, 1, axis=1)
        leading_device = jnp.stack([rolled[0], flipped[1]], 0)
        return jnp.where(inner_idx == 0, leading_device, flipped[::-1])

    def times_kernel_conj(kern, spec):
        return jnp.stack(
            [kern[0] * spec[0] + kern[1] * spec[1], kern[0] * spec[1] - kern[1] * spec[0]], 0
        )

    positions = (inner_idx * tok_dev + tok_range).astype(jnp.float32)
    rate_wide = decay_rate[:, None, :]
    coeff_wide = mode_coeff[:, None, :]
    to_end_pow = jnp.exp(-rate_wide * (group_len - 1.0 - positions)[None, :, None])
    from_start_pow = coeff_wide * jnp.exp(-rate_wide * (positions + 1.0)[None, :, None])
    tail_part = jnp.sum(coeff_wide * jnp.exp(-rate_wide * positions[None, :, None]), 0)
    group_decay = jnp.exp(-decay_rate * float(group_len))
    keep_full = jnp.concatenate(
        [boundary_keep, jnp.ones((1,) + boundary_keep.shape[1:], jnp.float32)], 0
    )
    keep_row = lax.dynamic_index_in_dim(keep_full, ctx_idx, 0, keepdims=False)
    link_decay = keep_row * group_decay
    kernel = filter_taps + tail_part
    kern_spec = to_spectrum((kernel,))
    mix_grad = cotangent * gate_input
    packed = to_spectrum((value_input, mix_grad))
    mirror_real = mirror_rows(packed[0])
    mirror_imag = mirror_rows(packed[1])
    val_spec = jnp.stack([0.5 * (packed[0] + mirror_real), 0.5 * (packed[1] - mirror_imag)], 0)
    grad_spec = jnp.stack([0.5 * (packed[1] + mirror_imag), 0.5 * (mirror_real - packed[0])], 0)
    ahead = jnp.stack(
        [
            kern_spec[0] * val_spec[0] - kern_spec[1] * val_spec[1],
            kern_spec[0] * val_spec[1] + kern_spec[1] * val_spec[0],
        ],
        0,
    )
    behind = times_kernel_conj(kern_spec, grad_spec)
    both_parts = from_spectrum(jnp.stack([ahead[0] - behind[1], ahead[1] + behind[0]], 0), True)
    inside = both_parts[0]
    through = both_parts[1]
    local_sums = jnp.sum(to_end_pow * value_input[None], 1)
    starts = carried_mode_state(link_decay, keep_row * local_sums, False)
    mixture = inside + jnp.sum(from_start_pow * starts[:, None, :], 0)
    mixed_out = gate_input * mixture
    grad_gate = cotangent * mixture
    pull_terms = jnp.sum(from_start_pow * mix_grad[None], 1)
    later_state = carried_mode_state(link_decay, pull_terms, True)
    grad_value = through + jnp.sum(to_end_pow * (keep_row * later_state)[:, None, :], 0)
    corr = times_kernel_conj(val_spec, grad_spec)
    share_spec = lax.psum_scatter(corr, "ctx", scatter_dimension=3, tiled=True)
    share_grad = from_spectrum(share_spec, False)[0]
    grad_filter = lax.all_gather(share_grad, "ctx", axis=1, tiled=True)
    grad_scale = 1.0 / math.sqrt(group_len * ctx_count)
    return (mixed_out, grad_gate, grad_value, grad_filter * grad_scale)


LANES = 128
SUBLANES = 8


def plus(x, y):
    return tuple(q if p is None else p if q is None else p + q for p, q in zip(x, y))


def minus(x, y):
    return tuple(
        p if q is None else -q if p is None else p - q for p, q in zip(x, y)
    )


def scaled(part, factor):
    if part is None or abs(factor) < 1e-12:
        return None
    if abs(factor - 1.0) < 1e-12:
        return part
    if abs(factor + 1.0) < 1e-12:
        return -part
    return part * factor


def turned(x, angle):
    c, s = math.cos(angle), math.sin(angle)
    real = minus((scaled(x[0], c),), (scaled(x[1], s),))[0] if x[1] is not None else scaled(x[0], c)
    imag = plus((scaled(x[0], s),), (scaled(x[1], c),))[0]
    return (real, imag)


def transform_ahead(xs):
    n = len(xs)
    if n == 1:
        return xs
    h = n // 2
    total = [plus(xs[i], xs[i + h]) for i in range(h)]
    apart = [turned(minus(xs[i], xs[i + h]), -2.0 * math.pi * i / n) for i in range(h)]
    even, odd = transform_ahead(total), transform_ahead(apart)
    return [(even, odd)[k % 2][k // 2] for k in range(n)]


def transform_behind(xs):
    n = len(xs)
    if n == 1:
        return xs
    h = n // 2
    even, odd = transform_behind(xs[0::2]), transform_behind(xs[1::2])
    odd = [turned(odd[i], 2.0 * math.pi * i / n) for i in range(h)]
    return [plus(even[i], odd[i]) for i in range(h)] + [minus(even[i], odd[i]) for i in range(h)]


def line_tables(width, row_count, half):
    turn = 2.0 * np.pi / width * (np.outer(np.arange(width), np.arange(width)) % width)
    c, s = np.cos(turn), np.sin(turn)
    line = np.concatenate([c, s], 1).astype(np.float32)
    length = width * row_count
    phase = 2.0 * np.pi / length * np.outer(np.arange(half), np.arange(width))
    weight = np.full((half, 1), 2.0)
    weight[0] = weight[-1] = 1.0
    twist = np.stack(
        [np.cos(phase), np.sin(phase), np.cos(phase) * weight / length, np.sin(phase) * weight / length]
    ).astype(np.float32)
    return line, twist


def mixer_kernel(
    ctx_count,
    inner_count,
    modes,
    gate_hbm,
    value_hbm,
    taps_hbm,
    rate_hbm,
    coeff_hbm,
    keep_hbm,
    cot_hbm,
    circle_hbm,
    twist_hbm,
    mixed_hbm,
    gated_hbm,
    turned_hbm,
    filtered_hbm,
    gate,
    value,
    taps,
    rate,
    coeff,
    keep,
    cot,
    circle,
    twist,
    ahead_high,
    ahead_low,
    behind_high,
    behind_low,
    send_taps,
    send_value,
    send_grad,
    got_taps,
    got_value,
    got_grad,
    spec,
    params,
    out_mix,
    out_through,
    out_corr,
    back_mix,
    back_through,
    back_corr,
    mixed_out,
    grad_gate,
    grad_value,
    grad_filter,
    load_sems,
    store_sems,
    send_sems,
    recv_sems,
):
    n = ctx_count * inner_count
    width = value.shape[0]
    chans = send_value.shape[1]
    chunks = chans // SUBLANES
    row_count = 2 * inner_count
    half = inner_count + 1
    group_len = width * inner_count
    ctx_idx = lax.axis_index("ctx")
    inner_idx = lax.axis_index("inner")
    me = ctx_idx * inner_count + inner_idx

    pairs = (
        (taps_hbm, taps),
        (value_hbm, value),
        (gate_hbm, gate),
        (cot_hbm, cot),
        (rate_hbm, rate),
        (coeff_hbm, coeff),
        (keep_hbm, keep),
        (twist_hbm, twist),
        (circle_hbm, circle),
    )
    loads = [
        pltpu.make_async_copy(src, dst, load_sems.at[i]) for i, (src, dst) in enumerate(pairs)
    ]
    for load in loads:
        load.start()

    barrier = pltpu.get_barrier_semaphore()

    def greet(k, carry):
        d = lax.rem(me + k, n)
        pl.semaphore_signal(
            barrier,
            inc=1,
            device_id=(lax.div(d, inner_count), lax.rem(d, inner_count)),
            device_id_type=pl.DeviceIdType.MESH,
        )
        return carry

    lax.fori_loop(1, n, greet, 0)

    def copy_to(src, dst, kind, d):
        return pltpu.make_async_remote_copy(
            src_ref=src,
            dst_ref=dst,
            send_sem=send_sems.at[kind],
            recv_sem=recv_sems.at[kind],
            device_id=(lax.div(d, inner_count), lax.rem(d, inner_count)),
            device_id_type=pl.DeviceIdType.MESH,
        )

    def exchange(src, dst, kind, partners, copy):
        def start(k, carry):
            copy(k).start()
            return carry

        every = pl.ds(0, partners)
        whole = copy_to(src.at[every], dst.at[every], kind, lax.rem(me + 1, n))
        return functools.partial(lax.fori_loop, 1, partners + 1, start, 0), whole

    def everyone(src, dst, kind):
        def copy(k):
            d = lax.rem(me + k, n)
            return copy_to(src.at[d], dst.at[me], kind, d)

        return exchange(src, dst, kind, n - 1, copy)

    def own_group(src, dst, kind):
        def copy(k):
            d = ctx_idx * inner_count + lax.rem(inner_idx + k, inner_count)
            return copy_to(src.at[d], dst.at[inner_idx], kind, d)

        return exchange(src, dst, kind, inner_count - 1, copy)

    def folded(src, dst, kind):
        def copy(k):
            d = lax.rem(me + k, n)
            return copy_to(src.at[lax.rem(d, inner_count)], dst.at[me], kind, d)

        return exchange(dst, dst, kind, n - 1, copy)

    taps_start, taps_all = own_group(send_taps, got_taps, 0)
    value_start, value_all = everyone(send_value, got_value, 1)
    grad_start, grad_all = everyone(send_grad, got_grad, 2)
    corr_start, corr_all = folded(out_corr, back_corr, 3)
    mix_start, mix_all = everyone(out_mix, back_mix, 4)
    through_start, through_all = everyone(out_through, back_through, 5)

    def by_channel(block):
        return jnp.transpose(block).reshape(n, chans, width)

    loads[0].wait()
    send_taps[...] = by_channel(taps[...])
    pl.semaphore_wait(barrier, n - 1)
    taps_start()
    got_taps[inner_idx] = send_taps[me]
    loads[1].wait()
    send_value[...] = by_channel(value[...])
    value_start()
    got_value[me] = send_value[me]
    loads[2].wait()
    loads[3].wait()
    send_grad[...] = by_channel(cot[...] * gate[...])
    grad_start()
    got_grad[me] = send_grad[me]

    for load in loads[4:]:
        load.wait()
    rows = [rate[...], coeff[...], keep[...]]
    filled = sum(r.shape[0] for r in rows)
    rows.append(jnp.zeros((LANES - filled, rate.shape[1]), jnp.float32))
    params[...] = jnp.transpose(jnp.concatenate(rows, 0))
    cosine, sine = circle[:, :width], circle[:, width:]
    for high, low, sign in ((ahead_high, ahead_low, 1.0), (behind_high, behind_low, -1.0)):
        table = jnp.concatenate(
            [
                jnp.concatenate([cosine, -sign * sine], 1),
                jnp.concatenate([sign * sine, cosine], 1),
            ],
            0,
        )
        top = table.astype(jnp.bfloat16)
        high[...] = top
        low[...] = (table - top.astype(jnp.float32)).astype(jnp.bfloat16)
    spec[:, half] = jnp.zeros(spec.shape[:1] + spec.shape[2:], jnp.float32)

    lane = lax.broadcasted_iota(jnp.int32, (SUBLANES, width), 1).astype(jnp.float32)

    def per_channel(chunk):
        own = params[pl.ds(pl.multiple_of(me * chans + chunk * SUBLANES, SUBLANES), SUBLANES), :]

        def wide(column):
            return jnp.broadcast_to(own[:, column : column + 1], (SUBLANES, width))

        rates = [wide(m) for m in range(modes)]
        coeffs = [wide(modes + m) for m in range(modes)]
        keeps = [
            [wide((2 + g) * modes + m) for m in range(modes)] for g in range(ctx_count - 1)
        ]
        return rates, coeffs, keeps

    def rows_of(chunk):
        return pl.ds(pl.multiple_of(chunk * SUBLANES, SUBLANES), SUBLANES)

    def add_tail(chunk, carry):
        rates, coeffs, _ = per_channel(chunk)
        steps = [jnp.exp(-r * float(width)) for r in rates]
        terms = [c * jnp.exp(-r * lane) for r, c in zip(rates, coeffs)]
        at = rows_of(chunk)
        for i in range(inner_count):
            got_taps[i, at, :] = got_taps[i, at, :] + sum(terms[1:], terms[0])
            terms = [t * s for t, s in zip(terms, steps)]
        return carry

    def rows_ahead(src, base, slot, chunk):
        at = rows_of(chunk)
        blank = (None, None)
        xs = [(src[base + i, at, :], None) for i in range(inner_count)] + [blank] * inner_count
        parts = transform_ahead(xs)
        for k in range(half):
            real, imag = parts[k]
            c, s = twist[0, k : k + 1, :], twist[1, k : k + 1, :]
            if imag is None:
                first, second = real * c, -(real * s)
            else:
                first, second = real * c + imag * s, imag * c - real * s
            spec[slot, k, at, :width] = first
            spec[slot, k, at, width:] = second

    def line(slot, high, low):
        data = spec[slot].reshape((half + 1) * chans, 2 * width)
        top = data.astype(jnp.bfloat16)
        rest = (data - top.astype(jnp.float32)).astype(jnp.bfloat16)
        dot = functools.partial(jnp.dot, preferred_element_type=jnp.float32)
        result = dot(rest, high[...]) + dot(top, low[...]) + dot(top, high[...])
        spec[slot] = result.reshape(half + 1, chans, 2 * width)

    def rows_behind(slot, chunk):
        at = rows_of(chunk)
        xs = []
        for k in range(half):
            real, imag = spec[slot, k, at, :width], spec[slot, k, at, width:]
            c, s = twist[2, k : k + 1, :], twist[3, k : k + 1, :]
            xs.append((real * c - imag * s, real * s + imag * c))
        xs += [(None, None)] * (row_count - half)
        return [y[0] for y in transform_behind(xs)[:inner_count]]

    def to_spectra(src, first_slot, groups):
        def one(step, carry):
            g = lax.div(step, chunks)
            rows_ahead(src, g * inner_count, first_slot + g, lax.rem(step, chunks))
            return carry

        lax.fori_loop(0, groups * chunks, one, 0)

        def transform(g, carry):
            line(first_slot + g, ahead_high, ahead_low)
            return carry

        lax.fori_loop(0, groups, transform, 0)

    taps_all.wait_recv()
    lax.fori_loop(0, chunks, add_tail, 0)
    kern_slot, value_slot, grad_slot = 0, 1, 1 + ctx_count
    to_spectra(got_taps, kern_slot, 1)
    value_all.wait_recv()
    to_spectra(got_value, value_slot, ctx_count)
    grad_all.wait_recv()
    to_spectra(got_grad, grad_slot, ctx_count)

    def multiply(step, carry):
        k = lax.div(step, chunks)
        at = rows_of(lax.rem(step, chunks))

        def load(slot):
            return spec[slot, k, at, :width], spec[slot, k, at, width:]

        def store(slot, real, imag):
            spec[slot, k, at, :width] = real
            spec[slot, k, at, width:] = imag

        kr, ki = load(kern_slot)
        corr_r = corr_i = 0.0
        for g in range(ctx_count):
            vr, vi = load(value_slot + g)
            gr, gi = load(grad_slot + g)
            corr_r = corr_r + (vr * gr + vi * gi)
            corr_i = corr_i + (vr * gi - vi * gr)
            store(value_slot + g, kr * vr - ki * vi, kr * vi + ki * vr)
            store(grad_slot + g, kr * gr + ki * gi, kr * gi - ki * gr)
        store(kern_slot, corr_r, corr_i)
        return carry

    lax.fori_loop(0, half * chunks, multiply, 0)

    grad_scale = 1.0 / math.sqrt(group_len * ctx_count)
    line(kern_slot, behind_high, behind_low)

    def corr_rows(chunk, carry):
        for i, y in enumerate(rows_behind(kern_slot, chunk)):
            out_corr[i, rows_of(chunk), :] = y * grad_scale
        return carry

    lax.fori_loop(0, chunks, corr_rows, 0)
    corr_start()
    back_corr[me] = out_corr[inner_idx]

    def from_spectra(first_slot, dst):
        def transform(g, carry):
            line(first_slot + g, behind_high, behind_low)
            return carry

        lax.fori_loop(0, ctx_count, transform, 0)

        def one(step, carry):
            g, chunk = lax.div(step, chunks), lax.rem(step, chunks)
            for i, y in enumerate(rows_behind(first_slot + g, chunk)):
                dst[g * inner_count + i, rows_of(chunk), :] = y
            return carry

        lax.fori_loop(0, ctx_count * chunks, one, 0)

    def carried_ahead(chunk, carry):
        rates, coeffs, keeps = per_channel(chunk)
        at = rows_of(chunk)
        steps = [jnp.exp(-r * float(width)) for r in rates]
        whole = [jnp.exp(-r * float(group_len)) for r in rates]
        to_end = [jnp.exp(-r * (width - 1.0 - lane)) for r in rates]
        from_start = [c * jnp.exp(-r * (lane + 1.0)) for r, c in zip(rates, coeffs)]
        state = [jnp.zeros((SUBLANES, 1), jnp.float32)] * modes
        for g in range(ctx_count - 1):
            acc = [jnp.zeros((SUBLANES, width), jnp.float32)] * modes
            for i in range(inner_count):
                block = got_value[g * inner_count + i, at, :]
                acc = [a * s + block for a, s in zip(acc, steps)]
            for m in range(modes):
                total = jnp.sum(acc[m] * to_end[m], 1, keepdims=True)
                state[m] = keeps[g][m][:, :1] * (whole[m][:, :1] * state[m] + total)
            terms = [f * st for f, st in zip(from_start, state)]
            for i in range(inner_count):
                row = (g + 1) * inner_count + i
                out_mix[row, at, :] = out_mix[row, at, :] + sum(terms[1:], terms[0])
                terms = [t * s for t, s in zip(terms, steps)]
        return carry

    def carried_behind(chunk, carry):
        rates, coeffs, keeps = per_channel(chunk)
        at = rows_of(chunk)
        steps = [jnp.exp(-r * float(width)) for r in rates]
        whole = [jnp.exp(-r * float(group_len)) for r in rates]
        to_end = [jnp.exp(-r * (width - 1.0 - lane)) for r in rates]
        from_start = [c * jnp.exp(-r * (lane + 1.0)) for r, c in zip(rates, coeffs)]
        state = [jnp.zeros((SUBLANES, 1), jnp.float32)] * modes
        for g in reversed(range(1, ctx_count)):
            acc = [jnp.zeros((SUBLANES, width), jnp.float32)] * modes
            for i in reversed(range(inner_count)):
                block = got_grad[g * inner_count + i, at, :]
                acc = [a * s + block for a, s in zip(acc, steps)]
            for m in range(modes):
                total = jnp.sum(acc[m] * from_start[m], 1, keepdims=True)
                if g < ctx_count - 1:
                    state[m] = total + whole[m][:, :1] * keeps[g][m][:, :1] * state[m]
                else:
                    state[m] = total
            terms = [
                t * (kp[:, :1] * st) for t, kp, st in zip(to_end, keeps[g - 1], state)
            ]
            for i in reversed(range(inner_count)):
                row = (g - 1) * inner_count + i
                out_through[row, at, :] = out_through[row, at, :] + sum(terms[1:], terms[0])
                terms = [t * s for t, s in zip(terms, steps)]
        return carry

    from_spectra(value_slot, out_mix)
    lax.fori_loop(0, chunks, carried_ahead, 0)
    mix_start()
    back_mix[me] = out_mix[me]
    from_spectra(grad_slot, out_through)
    lax.fori_loop(0, chunks, carried_behind, 0)
    through_start()
    back_through[me] = out_through[me]

    def by_token(blocks):
        return jnp.transpose(blocks[...].reshape(n * chans, width))

    corr_all.wait_recv()
    stores = [
        pltpu.make_async_copy(src, dst, store_sems.at[i])
        for i, (src, dst) in enumerate(
            (
                (mixed_out, mixed_hbm),
                (grad_gate, gated_hbm),
                (grad_value, turned_hbm),
                (grad_filter, filtered_hbm),
            )
        )
    ]
    grad_filter[...] = by_token(back_corr)
    stores[3].start()
    mix_all.wait_recv()
    mixture = by_token(back_mix)
    mixed_out[...] = gate[...] * mixture
    stores[0].start()
    grad_gate[...] = cot[...] * mixture
    stores[1].start()
    through_all.wait_recv()
    grad_value[...] = by_token(back_through)
    stores[2].start()
    for whole in (taps_all, value_all, grad_all, corr_all, mix_all, through_all):
        whole.wait_send()
    for store in stores:
        store.wait()


def finish_kernel(pieces, *refs):
    sources, targets, sems = refs[:4], refs[4:8], refs[8]
    rows = sources[0].shape[0] // pieces
    copies = [
        pltpu.make_async_copy(
            src.at[pl.ds(p * rows, rows)], dst.at[pl.ds(p * rows, rows)], sems.at[i, p]
        )
        for i, (src, dst) in enumerate(zip(sources, targets))
        for p in range(pieces)
    ]
    for copy in copies:
        copy.start()
    for copy in copies:
        copy.wait()


def fits(mesh, value_input):
    inner_count, ctx_count = mesh.shape["inner"], mesh.shape["ctx"]
    tok_dev, channels = value_input.shape
    return (
        tok_dev == LANES
        and channels % (inner_count * ctx_count * SUBLANES) == 0
        and inner_count & (inner_count - 1) == 0
    )


def shards_by_channel(
    mesh, gate_input, value_input, filter_taps, decay_rate, mode_coeff, boundary_keep, cotangent
):
    inner_count, ctx_count = mesh.shape["inner"], mesh.shape["ctx"]
    n = inner_count * ctx_count
    tok_dev, channels = value_input.shape
    modes = decay_rate.shape[0]
    chans = channels // n
    half = inner_count + 1
    tables = line_tables(tok_dev, 2 * inner_count, half)
    keep_rows = boundary_keep.reshape(-1, channels)
    block = jax.ShapeDtypeStruct((tok_dev, channels), jnp.float32)
    f32 = functools.partial(pltpu.VMEM, dtype=jnp.float32)
    pieces, own_pieces = f32((n, chans, tok_dev)), f32((inner_count, chans, tok_dev))
    hbm = pl.BlockSpec(memory_space=pltpu.HBM)
    operands = (
        gate_input,
        value_input,
        filter_taps,
        decay_rate,
        mode_coeff,
        keep_rows,
        cotangent,
        *tables,
    )
    results = pl.pallas_call(
        functools.partial(mixer_kernel, ctx_count, inner_count, modes),
        out_shape=(block,) * 4,
        in_specs=[hbm] * len(operands),
        out_specs=(hbm,) * 4,
        scratch_shapes=[pltpu.VMEM(a.shape, a.dtype) for a in operands]
        + [pltpu.VMEM((2 * tok_dev, 2 * tok_dev), jnp.bfloat16)] * 4
        + [
            pieces,
            pieces,
            pieces,
            own_pieces,
            pieces,
            pieces,
            f32((1 + 2 * ctx_count, half + 1, chans, 2 * tok_dev)),
            f32((channels, LANES)),
            pieces,
            pieces,
            own_pieces,
            pieces,
            pieces,
            pieces,
        ]
        + [f32((tok_dev, channels))] * 4
        + [
            pltpu.SemaphoreType.DMA((len(operands),)),
            pltpu.SemaphoreType.DMA((4,)),
            pltpu.SemaphoreType.DMA((6,)),
            pltpu.SemaphoreType.DMA((6,)),
        ],
        compiler_params=pltpu.CompilerParams(
            collective_id=0, has_side_effects=True, vmem_limit_bytes=60 * 1024 * 1024
        ),
    )(*operands)
    return pl.pallas_call(
        functools.partial(finish_kernel, 2),
        out_shape=(block,) * 4,
        in_specs=[hbm] * 4,
        out_specs=(hbm,) * 4,
        scratch_shapes=[pltpu.SemaphoreType.DMA((4, 2))],
        compiler_params=pltpu.CompilerParams(vmem_limit_bytes=60 * 1024 * 1024),
    )(*results)


def shards_of(mesh, *args):
    if fits(mesh, args[1]):
        return shards_by_channel(mesh, *args)
    return shards(*args)


def solution(mesh):
    placed = (
        P(("ctx", "inner"), None),
        P(("ctx", "inner"), None),
        P("inner", None),
        P(),
        P(),
        P(),
        P(("ctx", "inner"), None),
    )
    return jax.shard_map(
        functools.partial(shards_of, mesh),
        mesh=mesh,
        in_specs=placed,
        out_specs=(
            P(("ctx", "inner"), None),
            P(("ctx", "inner"), None),
            P(("ctx", "inner"), None),
            P("inner", None),
        ),
        check_vma=False,
    )
```

```python
import functools
import math

import jax
import jax.numpy as jnp
import numpy as np
from jax import lax
from jax.experimental import pallas as pl
from jax.experimental.pallas import tpu as pltpu
from jax.sharding import PartitionSpec as P

FULL_PRECISION = lax.Precision.HIGHEST


def prefix(part, axis, combine, identity, reverse):
    count = lax.axis_size(axis)
    place = lax.axis_index(axis)
    ahead = count - 1 - place if reverse else place
    gathered = jax.tree.map(lambda a: lax.all_gather(a, axis), part)
    state = jax.tree.map(lambda a, e: jnp.zeros_like(a) + jnp.asarray(e, a.dtype), part, identity)

    def one(hop, state):
        source = count - 1 - hop if reverse else hop
        return combine(
            state, jax.tree.map(lambda a: lax.dynamic_index_in_dim(a, source, 0, False), gathered)
        )

    return lax.fori_loop(0, ahead, one, state)


def turn_table(left_index, right_index, period):
    phase = (left_index * right_index % period).astype(jnp.float32) * (2.0 * math.pi / period)
    return (jnp.cos(phase), jnp.sin(phase))


def ahead_table(cosine, sine):
    return jnp.stack([jnp.stack([cosine, sine], 0), jnp.stack([-sine, cosine], 0)], 0)


def behind_table(cosine, sine):
    return jnp.stack([jnp.stack([cosine, -sine], 0), jnp.stack([sine, cosine], 0)], 0)


def contract(form, table, data):
    return jnp.einsum(form, table, data, precision=FULL_PRECISION)


def combine_links(earlier, later_link):
    return (later_link[0] * earlier[0], later_link[0] * earlier[1] + later_link[1])


def carried_mode_state(decay_factors, partial_terms, backward_pass):
    unit_links = jnp.ones_like(decay_factors)
    blank_terms = jnp.zeros_like(partial_terms)
    summed_total = lax.psum(partial_terms, "inner")
    return prefix(
        (decay_factors, summed_total),
        "ctx",
        combine_links,
        (unit_links, blank_terms),
        backward_pass,
    )[1]


def shards(gate_input, value_input, filter_taps, decay_rate, mode_coeff, boundary_keep, cotangent):
    tok_dev = value_input.shape[0]
    inner_count = lax.axis_size("inner")
    ctx_count = lax.axis_size("ctx")
    group_len = tok_dev * inner_count
    fft_len = 2 * group_len
    row_count = 2 * inner_count
    col_count = tok_dev // inner_count
    inner_idx = lax.axis_index("inner")
    ctx_idx = lax.axis_index("ctx")
    row_range = jnp.arange(row_count, dtype=jnp.int32)
    inner_range = jnp.arange(inner_count, dtype=jnp.int32)
    tok_range = jnp.arange(tok_dev, dtype=jnp.int32)
    owner_of_row = row_range // 2
    mirrored_label = jnp.where(owner_of_row == 0, inner_count, row_count - owner_of_row)
    row_label = jnp.where(row_range % 2 == 0, owner_of_row, mirrored_label)
    cos_rows, sin_rows = turn_table(row_label[:, None], inner_range[None, :], row_count)
    rows_table = ahead_table(cos_rows, sin_rows)
    col_index = inner_idx * col_count + jnp.arange(col_count, dtype=jnp.int32)
    cos_twist, sin_twist = turn_table(row_label[:, None, None], col_index[None, :, None], fft_len)
    cos_line, sin_line = turn_table(tok_range[:, None], tok_range[None, :], tok_dev)
    line_ahead = ahead_table(cos_line, sin_line)
    line_behind = behind_table(cos_line, sin_line)
    own_rows = lax.dynamic_slice_in_dim(row_label, 2 * inner_idx, 2, 0)
    cos_untwist, sin_untwist = turn_table(
        own_rows[:, None, None], tok_range[None, :, None], fft_len
    )
    cos_back, sine_reverse = turn_table(inner_range[:, None], row_label[None, :], row_count)
    back_table = behind_table(cos_back, sine_reverse)

    def to_spectrum(signals):
        stacked = jnp.stack(signals, 0)[:, None]
        columns = lax.all_to_all(stacked, "inner", split_axis=2, concat_axis=1, tiled=True)
        count = len(signals)
        parts = contract("pqki,qijc->pkjc", rows_table[:, :count], columns)
        turned = jnp.stack(
            [
                parts[0] * cos_twist + parts[1] * sin_twist,
                parts[1] * cos_twist - parts[0] * sin_twist,
            ],
            0,
        )
        spread = lax.all_to_all(turned, "inner", split_axis=1, concat_axis=2, tiled=True)
        return contract("pqkj,qbjc->pbkc", line_ahead, spread)

    def from_spectrum(spec, keep_imag):
        line = contract("pqjk,qbkc->pbjc", line_behind, spec)
        turned = jnp.stack(
            [
                line[0] * cos_untwist - line[1] * sin_untwist,
                line[1] * cos_untwist + line[0] * sin_untwist,
            ],
            0,
        )
        back = lax.all_to_all(turned, "inner", split_axis=2, concat_axis=1, tiled=True)
        count = 2 if keep_imag else 1
        row_values = contract("pqik,qkjc->pijc", back_table[:count], back) * (1.0 / fft_len)
        joined = lax.all_to_all(row_values, "inner", split_axis=1, concat_axis=2, tiled=True)
        return joined[:, 0]

    def mirror_rows(spec):
        flipped = spec[:, ::-1]
        rolled = jnp.roll(flipped, 1, axis=1)
        leading_device = jnp.stack([rolled[0], flipped[1]], 0)
        return jnp.where(inner_idx == 0, leading_device, flipped[::-1])

    def times_kernel_conj(kern, spec):
        return jnp.stack(
            [kern[0] * spec[0] + kern[1] * spec[1], kern[0] * spec[1] - kern[1] * spec[0]], 0
        )

    positions = (inner_idx * tok_dev + tok_range).astype(jnp.float32)
    rate_wide = decay_rate[:, None, :]
    coeff_wide = mode_coeff[:, None, :]
    to_end_pow = jnp.exp(-rate_wide * (group_len - 1.0 - positions)[None, :, None])
    from_start_pow = coeff_wide * jnp.exp(-rate_wide * (positions + 1.0)[None, :, None])
    tail_part = jnp.sum(coeff_wide * jnp.exp(-rate_wide * positions[None, :, None]), 0)
    group_decay = jnp.exp(-decay_rate * float(group_len))
    keep_full = jnp.concatenate(
        [boundary_keep, jnp.ones((1,) + boundary_keep.shape[1:], jnp.float32)], 0
    )
    keep_row = lax.dynamic_index_in_dim(keep_full, ctx_idx, 0, keepdims=False)
    link_decay = keep_row * group_decay
    kernel = filter_taps + tail_part
    kern_spec = to_spectrum((kernel,))
    mix_grad = cotangent * gate_input
    packed = to_spectrum((value_input, mix_grad))
    mirror_real = mirror_rows(packed[0])
    mirror_imag = mirror_rows(packed[1])
    val_spec = jnp.stack([0.5 * (packed[0] + mirror_real), 0.5 * (packed[1] - mirror_imag)], 0)
    grad_spec = jnp.stack([0.5 * (packed[1] + mirror_imag), 0.5 * (mirror_real - packed[0])], 0)
    ahead = jnp.stack(
        [
            kern_spec[0] * val_spec[0] - kern_spec[1] * val_spec[1],
            kern_spec[0] * val_spec[1] + kern_spec[1] * val_spec[0],
        ],
        0,
    )
    behind = times_kernel_conj(kern_spec, grad_spec)
    both_parts = from_spectrum(jnp.stack([ahead[0] - behind[1], ahead[1] + behind[0]], 0), True)
    inside = both_parts[0]
    through = both_parts[1]
    local_sums = jnp.sum(to_end_pow * value_input[None], 1)
    starts = carried_mode_state(link_decay, keep_row * local_sums, False)
    mixture = inside + jnp.sum(from_start_pow * starts[:, None, :], 0)
    mixed_out = gate_input * mixture
    grad_gate = cotangent * mixture
    pull_terms = jnp.sum(from_start_pow * mix_grad[None], 1)
    later_state = carried_mode_state(link_decay, pull_terms, True)
    grad_value = through + jnp.sum(to_end_pow * (keep_row * later_state)[:, None, :], 0)
    corr = times_kernel_conj(val_spec, grad_spec)
    share_spec = lax.psum_scatter(corr, "ctx", scatter_dimension=3, tiled=True)
    share_grad = from_spectrum(share_spec, False)[0]
    grad_filter = lax.all_gather(share_grad, "ctx", axis=1, tiled=True)
    grad_scale = 1.0 / math.sqrt(group_len * ctx_count)
    return (mixed_out, grad_gate, grad_value, grad_filter * grad_scale)


LANES = 128
SUBLANES = 8


def plus(x, y):
    return tuple(q if p is None else p if q is None else p + q for p, q in zip(x, y))


def minus(x, y):
    return tuple(
        p if q is None else -q if p is None else p - q for p, q in zip(x, y)
    )


def scaled(part, factor):
    if part is None or abs(factor) < 1e-12:
        return None
    if abs(factor - 1.0) < 1e-12:
        return part
    if abs(factor + 1.0) < 1e-12:
        return -part
    return part * factor


def turned(x, angle):
    c, s = math.cos(angle), math.sin(angle)
    real = minus((scaled(x[0], c),), (scaled(x[1], s),))[0] if x[1] is not None else scaled(x[0], c)
    imag = plus((scaled(x[0], s),), (scaled(x[1], c),))[0]
    return (real, imag)


def transform_ahead(xs):
    n = len(xs)
    if n == 1:
        return xs
    h = n // 2
    total = [plus(xs[i], xs[i + h]) for i in range(h)]
    apart = [turned(minus(xs[i], xs[i + h]), -2.0 * math.pi * i / n) for i in range(h)]
    even, odd = transform_ahead(total), transform_ahead(apart)
    return [(even, odd)[k % 2][k // 2] for k in range(n)]


def transform_behind(xs):
    n = len(xs)
    if n == 1:
        return xs
    h = n // 2
    even, odd = transform_behind(xs[0::2]), transform_behind(xs[1::2])
    odd = [turned(odd[i], 2.0 * math.pi * i / n) for i in range(h)]
    return [plus(even[i], odd[i]) for i in range(h)] + [minus(even[i], odd[i]) for i in range(h)]


def line_tables(width, row_count, half):
    turn = 2.0 * np.pi / width * (np.outer(np.arange(width), np.arange(width)) % width)
    c, s = np.cos(turn), np.sin(turn)
    line = np.concatenate([c, s], 1).astype(np.float32)
    length = width * row_count
    phase = 2.0 * np.pi / length * np.outer(np.arange(half), np.arange(width))
    weight = np.full((half, 1), 2.0)
    weight[0] = weight[-1] = 1.0
    twist = np.stack(
        [np.cos(phase), np.sin(phase), np.cos(phase) * weight / length, np.sin(phase) * weight / length]
    ).astype(np.float32)
    return line, twist


def mixer_kernel(
    ctx_count,
    inner_count,
    modes,
    gate_hbm,
    value_hbm,
    taps_hbm,
    rate_hbm,
    coeff_hbm,
    keep_hbm,
    cot_hbm,
    circle_hbm,
    twist_hbm,
    mixed_hbm,
    gated_hbm,
    turned_hbm,
    filtered_hbm,
    gate,
    value,
    taps,
    rate,
    coeff,
    keep,
    cot,
    circle,
    twist,
    ahead_high,
    ahead_low,
    behind_high,
    behind_low,
    send,
    got,
    spec,
    params,
    out,
    back,
    mixed_out,
    grad_gate,
    grad_value,
    grad_filter,
    load_sems,
    store_sems,
    send_sems,
    recv_sems,
):
    n = ctx_count * inner_count
    width = value.shape[0]
    chunks = send.shape[0]
    span = n * SUBLANES
    row_count = 2 * inner_count
    half = inner_count + 1
    group_len = width * inner_count
    ctx_idx = lax.axis_index("ctx")
    inner_idx = lax.axis_index("inner")
    me = ctx_idx * inner_count + inner_idx

    pairs = (
        (taps_hbm, taps),
        (value_hbm, value),
        (gate_hbm, gate),
        (cot_hbm, cot),
        (rate_hbm, rate),
        (coeff_hbm, coeff),
        (keep_hbm, keep),
        (twist_hbm, twist),
        (circle_hbm, circle),
    )
    loads = [
        pltpu.make_async_copy(src, dst, load_sems.at[i]) for i, (src, dst) in enumerate(pairs)
    ]
    for load in loads:
        load.start()

    barrier = pltpu.get_barrier_semaphore()

    def greet(k, carry):
        d = lax.rem(me + k, n)
        pl.semaphore_signal(
            barrier,
            inc=1,
            device_id=(lax.div(d, inner_count), lax.rem(d, inner_count)),
            device_id_type=pl.DeviceIdType.MESH,
        )
        return carry

    lax.fori_loop(1, n, greet, 0)

    def copy_to(src, dst, kind, d):
        return pltpu.make_async_remote_copy(
            src_ref=src,
            dst_ref=dst,
            send_sem=send_sems.at[kind[0], kind[1]],
            recv_sem=recv_sems.at[kind[0], kind[1]],
            device_id=(lax.div(d, inner_count), lax.rem(d, inner_count)),
            device_id_type=pl.DeviceIdType.MESH,
        )

    rest = n - inner_count
    shared = pl.ds(0, 2)

    def start_in(c):
        def cross(k, carry):
            group = ctx_idx + 1 + lax.div(k, inner_count)
            d = lax.rem(group * inner_count + lax.rem(inner_idx + k, inner_count), n)
            copy_to(send.at[c, d, shared], got.at[c, me, shared], (1, c), d).start()
            return carry

        def own(k, carry):
            d = ctx_idx * inner_count + lax.rem(inner_idx + k, inner_count)
            copy_to(send.at[c, d], got.at[c, me], (0, c), d).start()
            return carry

        lax.fori_loop(0, rest, cross, 0)
        lax.fori_loop(1, inner_count, own, 0)

    def start_out(c):
        def one(k, carry):
            d = lax.rem(me + k, n)
            copy_to(out.at[c, d], back.at[c, me], (2, c), d).start()
            return carry

        lax.fori_loop(1, n, one, 0)

    other = lax.rem(me + 1, n)

    def all_in(c):
        few, many = pl.ds(0, inner_count - 1), pl.ds(0, rest)
        return (
            copy_to(send.at[c, few], got.at[c, few], (0, c), other),
            copy_to(send.at[c, many, shared], got.at[c, many, shared], (1, c), other),
        )

    def all_out(c):
        every = pl.ds(0, n - 1)
        return copy_to(out.at[c, every], back.at[c, every], (2, c), other)

    def by_channel(block):
        return jnp.transpose(block).reshape(n, SUBLANES, width)

    for load in loads[:4]:
        load.wait()
    for c in range(chunks):
        cols = slice(c * span, (c + 1) * span)
        send[c, :, 0] = by_channel(value[:, cols])
        send[c, :, 1] = by_channel(cot[:, cols] * gate[:, cols])
        send[c, :, 2] = by_channel(taps[:, cols])
        if c == 0:
            pl.semaphore_wait(barrier, n - 1)
        start_in(c)
        got[c, me] = send[c, me]

    for load in loads[4:]:
        load.wait()
    rows = [rate[...], coeff[...], keep[...]]
    filled = sum(r.shape[0] for r in rows)
    rows.append(jnp.zeros((LANES - filled, rate.shape[1]), jnp.float32))
    params[...] = jnp.transpose(jnp.concatenate(rows, 0))
    cosine, sine = circle[:, :width], circle[:, width:]
    for high, low, sign in ((ahead_high, ahead_low, 1.0), (behind_high, behind_low, -1.0)):
        table = jnp.concatenate(
            [
                jnp.concatenate([cosine, -sign * sine], 1),
                jnp.concatenate([sign * sine, cosine], 1),
            ],
            0,
        )
        top = table.astype(jnp.bfloat16)
        high[...] = top
        low[...] = (table - top.astype(jnp.float32)).astype(jnp.bfloat16)
    spec[:, half] = jnp.zeros(spec.shape[:1] + spec.shape[2:], jnp.float32)

    lane = lax.broadcasted_iota(jnp.int32, (SUBLANES, width), 1).astype(jnp.float32)

    def per_channel(chunk):
        own = params[pl.ds(pl.multiple_of(chunk * span + me * SUBLANES, SUBLANES), SUBLANES), :]

        def wide(column):
            return jnp.broadcast_to(own[:, column : column + 1], (SUBLANES, width))

        rates = [wide(m) for m in range(modes)]
        coeffs = [wide(modes + m) for m in range(modes)]
        keeps = [
            [wide((2 + g) * modes + m) for m in range(modes)] for g in range(ctx_count - 1)
        ]
        return rates, coeffs, keeps

    def add_tail(c):
        rates, coeffs, _ = per_channel(c)
        steps = [jnp.exp(-r * float(width)) for r in rates]
        terms = [f * jnp.exp(-r * lane) for r, f in zip(rates, coeffs)]
        base = ctx_idx * inner_count
        for i in range(inner_count):
            got[c, base + i, 2] = got[c, base + i, 2] + sum(terms[1:], terms[0])
            terms = [t * s for t, s in zip(terms, steps)]

    def rows_ahead(c, base, tensor, slot):
        blank = (None, None)
        xs = [(got[c, base + i, tensor], None) for i in range(inner_count)] + [blank] * inner_count
        parts = transform_ahead(xs)
        for k in range(half):
            real, imag = parts[k]
            cosine, sine = twist[0, k : k + 1, :], twist[1, k : k + 1, :]
            if imag is None:
                first, second = real * cosine, -(real * sine)
            else:
                first, second = real * cosine + imag * sine, imag * cosine - real * sine
            spec[slot, k, :, :width] = first
            spec[slot, k, :, width:] = second

    def lines(high, low):
        data = spec[...].reshape(-1, 2 * width)
        top = data.astype(jnp.bfloat16)
        rest_part = (data - top.astype(jnp.float32)).astype(jnp.bfloat16)
        dot = functools.partial(jnp.dot, preferred_element_type=jnp.float32)
        result = dot(rest_part, high[...]) + dot(top, low[...]) + dot(top, high[...])
        spec[...] = result.reshape(spec.shape)

    def rows_behind(slot):
        xs = []
        for k in range(half):
            real, imag = spec[slot, k, :, :width], spec[slot, k, :, width:]
            cosine, sine = twist[2, k : k + 1, :], twist[3, k : k + 1, :]
            xs.append((real * cosine - imag * sine, real * sine + imag * cosine))
        xs += [(None, None)] * (row_count - half)
        return [y[0] for y in transform_behind(xs)[:inner_count]]

    kern_slot, value_slot, grad_slot = 0, 1, 1 + ctx_count
    grad_scale = 1.0 / math.sqrt(group_len * ctx_count)

    def multiply(k, carry):
        def load(slot):
            return spec[slot, k, :, :width], spec[slot, k, :, width:]

        def store(slot, real, imag):
            spec[slot, k, :, :width] = real
            spec[slot, k, :, width:] = imag

        kr, ki = load(kern_slot)
        corr_r = corr_i = 0.0
        for g in range(ctx_count):
            vr, vi = load(value_slot + g)
            gr, gi = load(grad_slot + g)
            corr_r = corr_r + (vr * gr + vi * gi)
            corr_i = corr_i + (vr * gi - vi * gr)
            store(value_slot + g, kr * vr - ki * vi, kr * vi + ki * vr)
            store(grad_slot + g, kr * gr + ki * gi, kr * gi - ki * gr)
        store(kern_slot, corr_r, corr_i)
        return carry

    def carried_ahead(chunk):
        rates, coeffs, keeps = per_channel(chunk)
        steps = [jnp.exp(-r * float(width)) for r in rates]
        whole = [jnp.exp(-r * float(group_len)) for r in rates]
        to_end = [jnp.exp(-r * (width - 1.0 - lane)) for r in rates]
        from_start = [c * jnp.exp(-r * (lane + 1.0)) for r, c in zip(rates, coeffs)]
        state = [jnp.zeros((SUBLANES, 1), jnp.float32)] * modes
        for g in range(ctx_count - 1):
            acc = [jnp.zeros((SUBLANES, width), jnp.float32)] * modes
            for i in range(inner_count):
                block = got[chunk, g * inner_count + i, 0]
                acc = [a * s + block for a, s in zip(acc, steps)]
            for m in range(modes):
                total = jnp.sum(acc[m] * to_end[m], 1, keepdims=True)
                state[m] = keeps[g][m][:, :1] * (whole[m][:, :1] * state[m] + total)
            terms = [f * st for f, st in zip(from_start, state)]
            for i in range(inner_count):
                row = (g + 1) * inner_count + i
                out[chunk, row, 0] = out[chunk, row, 0] + sum(terms[1:], terms[0])
                terms = [t * s for t, s in zip(terms, steps)]

    def carried_behind(chunk):
        rates, coeffs, keeps = per_channel(chunk)
        steps = [jnp.exp(-r * float(width)) for r in rates]
        whole = [jnp.exp(-r * float(group_len)) for r in rates]
        to_end = [jnp.exp(-r * (width - 1.0 - lane)) for r in rates]
        from_start = [c * jnp.exp(-r * (lane + 1.0)) for r, c in zip(rates, coeffs)]
        state = [jnp.zeros((SUBLANES, 1), jnp.float32)] * modes
        for g in reversed(range(1, ctx_count)):
            acc = [jnp.zeros((SUBLANES, width), jnp.float32)] * modes
            for i in reversed(range(inner_count)):
                block = got[chunk, g * inner_count + i, 1]
                acc = [a * s + block for a, s in zip(acc, steps)]
            for m in range(modes):
                total = jnp.sum(acc[m] * from_start[m], 1, keepdims=True)
                if g < ctx_count - 1:
                    state[m] = total + whole[m][:, :1] * keeps[g][m][:, :1] * state[m]
                else:
                    state[m] = total
            terms = [
                t * (kp[:, :1] * st) for t, kp, st in zip(to_end, keeps[g - 1], state)
            ]
            for i in reversed(range(inner_count)):
                row = (g - 1) * inner_count + i
                out[chunk, row, 1] = out[chunk, row, 1] + sum(terms[1:], terms[0])
                terms = [t * s for t, s in zip(terms, steps)]

    def process(c, carry):
        for whole in all_in(c):
            whole.wait_recv()
        add_tail(c)
        rows_ahead(c, ctx_idx * inner_count, 2, kern_slot)

        def ahead(step, inner_carry):
            tensor, g = lax.div(step, ctx_count), lax.rem(step, ctx_count)
            rows_ahead(c, g * inner_count, tensor, 1 + step)
            return inner_carry

        lax.fori_loop(0, 2 * ctx_count, ahead, 0)
        lines(ahead_high, ahead_low)
        lax.fori_loop(0, half, multiply, 0)
        lines(behind_high, behind_low)
        for i, y in enumerate(rows_behind(kern_slot)):
            y = y * grad_scale
            for g in range(ctx_count):
                out[c, g * inner_count + i, 2] = y

        def behind(step, inner_carry):
            tensor, g = lax.div(step, ctx_count), lax.rem(step, ctx_count)
            for i, y in enumerate(rows_behind(1 + step)):
                out[c, g * inner_count + i, tensor] = y
            return inner_carry

        lax.fori_loop(0, 2 * ctx_count, behind, 0)
        carried_ahead(c)
        carried_behind(c)
        start_out(c)
        back[c, me] = out[c, me]
        return carry

    lax.fori_loop(0, chunks, process, 0)

    def by_token(c, tensor):
        return jnp.transpose(back[c, :, tensor].reshape(span, width))

    stores = []
    for c in range(chunks):
        cols = slice(c * span, (c + 1) * span)
        all_out(c).wait_recv()
        mixture = by_token(c, 0)
        mixed_out[:, cols] = gate[:, cols] * mixture
        grad_gate[:, cols] = cot[:, cols] * mixture
        grad_value[:, cols] = by_token(c, 1)
        grad_filter[:, cols] = by_token(c, 2)
        moves = (
            (mixed_out, mixed_hbm),
            (grad_gate, gated_hbm),
            (grad_value, turned_hbm),
            (grad_filter, filtered_hbm),
        )
        for i, (src, dst) in enumerate(moves):
            part = pl.ds(c * span, span)
            store = pltpu.make_async_copy(src.at[:, part], dst.at[:, part], store_sems.at[i, c])
            store.start()
            stores.append(store)
    for c in range(chunks):
        for whole in all_in(c) + (all_out(c),):
            whole.wait_send()
    for store in stores:
        store.wait()


def finish_kernel(*refs):
    sources, targets, held, load_sems, store_sems = refs[:4], refs[4:8], refs[8:12], refs[12], refs[13]
    loads = [
        pltpu.make_async_copy(src, mid, load_sems.at[i])
        for i, (src, mid) in enumerate(zip(sources, held))
    ]
    stores = [
        pltpu.make_async_copy(mid, dst, store_sems.at[i])
        for i, (mid, dst) in enumerate(zip(held, targets))
    ]
    for load in loads:
        load.start()
    for load, store in zip(loads, stores):
        load.wait()
        store.start()
    for store in stores:
        store.wait()


def fits(mesh, value_input):
    inner_count, ctx_count = mesh.shape["inner"], mesh.shape["ctx"]
    tok_dev, channels = value_input.shape
    return (
        tok_dev == LANES
        and ctx_count > 1
        and channels % (inner_count * ctx_count * SUBLANES) == 0
        and inner_count & (inner_count - 1) == 0
    )


def shards_by_channel(
    mesh, gate_input, value_input, filter_taps, decay_rate, mode_coeff, boundary_keep, cotangent
):
    inner_count, ctx_count = mesh.shape["inner"], mesh.shape["ctx"]
    n = inner_count * ctx_count
    tok_dev, channels = value_input.shape
    modes = decay_rate.shape[0]
    chunks = channels // (n * SUBLANES)
    half = inner_count + 1
    tables = line_tables(tok_dev, 2 * inner_count, half)
    keep_rows = boundary_keep.reshape(-1, channels)
    block = jax.ShapeDtypeStruct((tok_dev, channels), jnp.float32)
    f32 = functools.partial(pltpu.VMEM, dtype=jnp.float32)
    pieces = f32((chunks, n, 3, SUBLANES, tok_dev))
    hbm = pl.BlockSpec(memory_space=pltpu.HBM)
    operands = (
        gate_input,
        value_input,
        filter_taps,
        decay_rate,
        mode_coeff,
        keep_rows,
        cotangent,
        *tables,
    )
    results = pl.pallas_call(
        functools.partial(mixer_kernel, ctx_count, inner_count, modes),
        out_shape=(block,) * 4,
        in_specs=[hbm] * len(operands),
        out_specs=(hbm,) * 4,
        scratch_shapes=[pltpu.VMEM(a.shape, a.dtype) for a in operands]
        + [pltpu.VMEM((2 * tok_dev, 2 * tok_dev), jnp.bfloat16)] * 4
        + [
            pieces,
            pieces,
            f32((1 + 2 * ctx_count, half + 1, SUBLANES, 2 * tok_dev)),
            f32((channels, LANES)),
            pieces,
            pieces,
        ]
        + [f32((tok_dev, channels))] * 4
        + [
            pltpu.SemaphoreType.DMA((len(operands),)),
            pltpu.SemaphoreType.DMA((4, chunks)),
            pltpu.SemaphoreType.DMA((3, chunks)),
            pltpu.SemaphoreType.DMA((3, chunks)),
        ],
        compiler_params=pltpu.CompilerParams(
            collective_id=0, has_side_effects=True, vmem_limit_bytes=60 * 1024 * 1024
        ),
    )(*operands)
    return pl.pallas_call(
        finish_kernel,
        out_shape=(block,) * 4,
        in_specs=[hbm] * 4,
        out_specs=(hbm,) * 4,
        scratch_shapes=[f32((tok_dev, channels))] * 4
        + [pltpu.SemaphoreType.DMA((4,)), pltpu.SemaphoreType.DMA((4,))],
        compiler_params=pltpu.CompilerParams(vmem_limit_bytes=60 * 1024 * 1024),
    )(*results)


def shards_of(mesh, *args):
    if fits(mesh, args[1]):
        return shards_by_channel(mesh, *args)
    return shards(*args)


def solution(mesh):
    placed = (
        P(("ctx", "inner"), None),
        P(("ctx", "inner"), None),
        P("inner", None),
        P(),
        P(),
        P(),
        P(("ctx", "inner"), None),
    )
    return jax.shard_map(
        functools.partial(shards_of, mesh),
        mesh=mesh,
        in_specs=placed,
        out_specs=(
            P(("ctx", "inner"), None),
            P(("ctx", "inner"), None),
            P(("ctx", "inner"), None),
            P("inner", None),
        ),
        check_vma=False,
    )
```

```python
import functools
import math

import jax
import jax.numpy as jnp
import numpy as np
from jax import lax
from jax.experimental import pallas as pl
from jax.experimental.pallas import tpu as pltpu
from jax.sharding import PartitionSpec as P

FULL_PRECISION = lax.Precision.HIGHEST


def prefix(part, axis, combine, identity, reverse):
    count = lax.axis_size(axis)
    place = lax.axis_index(axis)
    ahead = count - 1 - place if reverse else place
    gathered = jax.tree.map(lambda a: lax.all_gather(a, axis), part)
    state = jax.tree.map(lambda a, e: jnp.zeros_like(a) + jnp.asarray(e, a.dtype), part, identity)

    def one(hop, state):
        source = count - 1 - hop if reverse else hop
        return combine(
            state, jax.tree.map(lambda a: lax.dynamic_index_in_dim(a, source, 0, False), gathered)
        )

    return lax.fori_loop(0, ahead, one, state)


def turn_table(left_index, right_index, period):
    phase = (left_index * right_index % period).astype(jnp.float32) * (2.0 * math.pi / period)
    return (jnp.cos(phase), jnp.sin(phase))


def ahead_table(cosine, sine):
    return jnp.stack([jnp.stack([cosine, sine], 0), jnp.stack([-sine, cosine], 0)], 0)


def behind_table(cosine, sine):
    return jnp.stack([jnp.stack([cosine, -sine], 0), jnp.stack([sine, cosine], 0)], 0)


def contract(form, table, data):
    return jnp.einsum(form, table, data, precision=FULL_PRECISION)


def combine_links(earlier, later_link):
    return (later_link[0] * earlier[0], later_link[0] * earlier[1] + later_link[1])


def carried_mode_state(decay_factors, partial_terms, backward_pass):
    unit_links = jnp.ones_like(decay_factors)
    blank_terms = jnp.zeros_like(partial_terms)
    summed_total = lax.psum(partial_terms, "inner")
    return prefix(
        (decay_factors, summed_total),
        "ctx",
        combine_links,
        (unit_links, blank_terms),
        backward_pass,
    )[1]


def shards(gate_input, value_input, filter_taps, decay_rate, mode_coeff, boundary_keep, cotangent):
    tok_dev = value_input.shape[0]
    inner_count = lax.axis_size("inner")
    ctx_count = lax.axis_size("ctx")
    group_len = tok_dev * inner_count
    fft_len = 2 * group_len
    row_count = 2 * inner_count
    col_count = tok_dev // inner_count
    inner_idx = lax.axis_index("inner")
    ctx_idx = lax.axis_index("ctx")
    row_range = jnp.arange(row_count, dtype=jnp.int32)
    inner_range = jnp.arange(inner_count, dtype=jnp.int32)
    tok_range = jnp.arange(tok_dev, dtype=jnp.int32)
    owner_of_row = row_range // 2
    mirrored_label = jnp.where(owner_of_row == 0, inner_count, row_count - owner_of_row)
    row_label = jnp.where(row_range % 2 == 0, owner_of_row, mirrored_label)
    cos_rows, sin_rows = turn_table(row_label[:, None], inner_range[None, :], row_count)
    rows_table = ahead_table(cos_rows, sin_rows)
    col_index = inner_idx * col_count + jnp.arange(col_count, dtype=jnp.int32)
    cos_twist, sin_twist = turn_table(row_label[:, None, None], col_index[None, :, None], fft_len)
    cos_line, sin_line = turn_table(tok_range[:, None], tok_range[None, :], tok_dev)
    line_ahead = ahead_table(cos_line, sin_line)
    line_behind = behind_table(cos_line, sin_line)
    own_rows = lax.dynamic_slice_in_dim(row_label, 2 * inner_idx, 2, 0)
    cos_untwist, sin_untwist = turn_table(
        own_rows[:, None, None], tok_range[None, :, None], fft_len
    )
    cos_back, sine_reverse = turn_table(inner_range[:, None], row_label[None, :], row_count)
    back_table = behind_table(cos_back, sine_reverse)

    def to_spectrum(signals):
        stacked = jnp.stack(signals, 0)[:, None]
        columns = lax.all_to_all(stacked, "inner", split_axis=2, concat_axis=1, tiled=True)
        count = len(signals)
        parts = contract("pqki,qijc->pkjc", rows_table[:, :count], columns)
        turned = jnp.stack(
            [
                parts[0] * cos_twist + parts[1] * sin_twist,
                parts[1] * cos_twist - parts[0] * sin_twist,
            ],
            0,
        )
        spread = lax.all_to_all(turned, "inner", split_axis=1, concat_axis=2, tiled=True)
        return contract("pqkj,qbjc->pbkc", line_ahead, spread)

    def from_spectrum(spec, keep_imag):
        line = contract("pqjk,qbkc->pbjc", line_behind, spec)
        turned = jnp.stack(
            [
                line[0] * cos_untwist - line[1] * sin_untwist,
                line[1] * cos_untwist + line[0] * sin_untwist,
            ],
            0,
        )
        back = lax.all_to_all(turned, "inner", split_axis=2, concat_axis=1, tiled=True)
        count = 2 if keep_imag else 1
        row_values = contract("pqik,qkjc->pijc", back_table[:count], back) * (1.0 / fft_len)
        joined = lax.all_to_all(row_values, "inner", split_axis=1, concat_axis=2, tiled=True)
        return joined[:, 0]

    def mirror_rows(spec):
        flipped = spec[:, ::-1]
        rolled = jnp.roll(flipped, 1, axis=1)
        leading_device = jnp.stack([rolled[0], flipped[1]], 0)
        return jnp.where(inner_idx == 0, leading_device, flipped[::-1])

    def times_kernel_conj(kern, spec):
        return jnp.stack(
            [kern[0] * spec[0] + kern[1] * spec[1], kern[0] * spec[1] - kern[1] * spec[0]], 0
        )

    positions = (inner_idx * tok_dev + tok_range).astype(jnp.float32)
    rate_wide = decay_rate[:, None, :]
    coeff_wide = mode_coeff[:, None, :]
    to_end_pow = jnp.exp(-rate_wide * (group_len - 1.0 - positions)[None, :, None])
    from_start_pow = coeff_wide * jnp.exp(-rate_wide * (positions + 1.0)[None, :, None])
    tail_part = jnp.sum(coeff_wide * jnp.exp(-rate_wide * positions[None, :, None]), 0)
    group_decay = jnp.exp(-decay_rate * float(group_len))
    keep_full = jnp.concatenate(
        [boundary_keep, jnp.ones((1,) + boundary_keep.shape[1:], jnp.float32)], 0
    )
    keep_row = lax.dynamic_index_in_dim(keep_full, ctx_idx, 0, keepdims=False)
    link_decay = keep_row * group_decay
    kernel = filter_taps + tail_part
    kern_spec = to_spectrum((kernel,))
    mix_grad = cotangent * gate_input
    packed = to_spectrum((value_input, mix_grad))
    mirror_real = mirror_rows(packed[0])
    mirror_imag = mirror_rows(packed[1])
    val_spec = jnp.stack([0.5 * (packed[0] + mirror_real), 0.5 * (packed[1] - mirror_imag)], 0)
    grad_spec = jnp.stack([0.5 * (packed[1] + mirror_imag), 0.5 * (mirror_real - packed[0])], 0)
    ahead = jnp.stack(
        [
            kern_spec[0] * val_spec[0] - kern_spec[1] * val_spec[1],
            kern_spec[0] * val_spec[1] + kern_spec[1] * val_spec[0],
        ],
        0,
    )
    behind = times_kernel_conj(kern_spec, grad_spec)
    both_parts = from_spectrum(jnp.stack([ahead[0] - behind[1], ahead[1] + behind[0]], 0), True)
    inside = both_parts[0]
    through = both_parts[1]
    local_sums = jnp.sum(to_end_pow * value_input[None], 1)
    starts = carried_mode_state(link_decay, keep_row * local_sums, False)
    mixture = inside + jnp.sum(from_start_pow * starts[:, None, :], 0)
    mixed_out = gate_input * mixture
    grad_gate = cotangent * mixture
    pull_terms = jnp.sum(from_start_pow * mix_grad[None], 1)
    later_state = carried_mode_state(link_decay, pull_terms, True)
    grad_value = through + jnp.sum(to_end_pow * (keep_row * later_state)[:, None, :], 0)
    corr = times_kernel_conj(val_spec, grad_spec)
    share_spec = lax.psum_scatter(corr, "ctx", scatter_dimension=3, tiled=True)
    share_grad = from_spectrum(share_spec, False)[0]
    grad_filter = lax.all_gather(share_grad, "ctx", axis=1, tiled=True)
    grad_scale = 1.0 / math.sqrt(group_len * ctx_count)
    return (mixed_out, grad_gate, grad_value, grad_filter * grad_scale)


LANES = 128
SUBLANES = 8


def plus(x, y):
    return tuple(q if p is None else p if q is None else p + q for p, q in zip(x, y))


def minus(x, y):
    return tuple(
        p if q is None else -q if p is None else p - q for p, q in zip(x, y)
    )


def scaled(part, factor):
    if part is None or abs(factor) < 1e-12:
        return None
    if abs(factor - 1.0) < 1e-12:
        return part
    if abs(factor + 1.0) < 1e-12:
        return -part
    return part * factor


def turned(x, angle):
    c, s = math.cos(angle), math.sin(angle)
    real = minus((scaled(x[0], c),), (scaled(x[1], s),))[0] if x[1] is not None else scaled(x[0], c)
    imag = plus((scaled(x[0], s),), (scaled(x[1], c),))[0]
    return (real, imag)


def transform_ahead(xs):
    n = len(xs)
    if n == 1:
        return xs
    h = n // 2
    total = [plus(xs[i], xs[i + h]) for i in range(h)]
    apart = [turned(minus(xs[i], xs[i + h]), -2.0 * math.pi * i / n) for i in range(h)]
    even, odd = transform_ahead(total), transform_ahead(apart)
    return [(even, odd)[k % 2][k // 2] for k in range(n)]


def transform_behind(xs):
    n = len(xs)
    if n == 1:
        return xs
    h = n // 2
    even, odd = transform_behind(xs[0::2]), transform_behind(xs[1::2])
    odd = [turned(odd[i], 2.0 * math.pi * i / n) for i in range(h)]
    return [plus(even[i], odd[i]) for i in range(h)] + [minus(even[i], odd[i]) for i in range(h)]


def line_tables(width, row_count, half):
    turn = 2.0 * np.pi / width * (np.outer(np.arange(width), np.arange(width)) % width)
    c, s = np.cos(turn), np.sin(turn)
    line = np.concatenate([c, s], 1).astype(np.float32)
    length = width * row_count
    phase = 2.0 * np.pi / length * np.outer(np.arange(half), np.arange(width))
    weight = np.full((half, 1), 2.0)
    weight[0] = weight[-1] = 1.0
    twist = np.stack(
        [np.cos(phase), np.sin(phase), np.cos(phase) * weight / length, np.sin(phase) * weight / length]
    ).astype(np.float32)
    return line, twist


def mixer_kernel(
    ctx_count,
    inner_count,
    modes,
    gate_hbm,
    value_hbm,
    taps_hbm,
    rate_hbm,
    coeff_hbm,
    keep_hbm,
    cot_hbm,
    circle_hbm,
    twist_hbm,
    mixed_hbm,
    gated_hbm,
    turned_hbm,
    filtered_hbm,
    gate,
    value,
    taps,
    rate,
    coeff,
    keep,
    cot,
    circle,
    twist,
    ahead_high,
    ahead_low,
    behind_high,
    behind_low,
    send,
    got,
    spec,
    params,
    out,
    back,
    mixed_out,
    grad_gate,
    grad_value,
    grad_filter,
    load_sems,
    store_sems,
    send_sems,
    recv_sems,
):
    n = ctx_count * inner_count
    width = value.shape[0]
    chunks = send.shape[0]
    span = n * SUBLANES
    row_count = 2 * inner_count
    half = inner_count + 1
    group_len = width * inner_count
    ctx_idx = lax.axis_index("ctx")
    inner_idx = lax.axis_index("inner")
    me = ctx_idx * inner_count + inner_idx

    pairs = (
        (taps_hbm, taps),
        (value_hbm, value),
        (gate_hbm, gate),
        (cot_hbm, cot),
        (rate_hbm, rate),
        (coeff_hbm, coeff),
        (keep_hbm, keep),
        (twist_hbm, twist),
        (circle_hbm, circle),
    )
    loads = [
        pltpu.make_async_copy(src, dst, load_sems.at[i]) for i, (src, dst) in enumerate(pairs)
    ]
    for load in loads:
        load.start()

    barrier = pltpu.get_barrier_semaphore()

    def greet(k, carry):
        d = lax.rem(me + k, n)
        pl.semaphore_signal(
            barrier,
            inc=1,
            device_id=(lax.div(d, inner_count), lax.rem(d, inner_count)),
            device_id_type=pl.DeviceIdType.MESH,
        )
        return carry

    lax.fori_loop(1, n, greet, 0)

    def copy_to(src, dst, kind, d):
        return pltpu.make_async_remote_copy(
            src_ref=src,
            dst_ref=dst,
            send_sem=send_sems.at[kind[0], kind[1]],
            recv_sem=recv_sems.at[kind[0], kind[1]],
            device_id=(lax.div(d, inner_count), lax.rem(d, inner_count)),
            device_id_type=pl.DeviceIdType.MESH,
        )

    rest = n - inner_count
    other = lax.rem(me + 1, n)

    def spread(src, dst, c, kind, tensors):
        def cross(k, carry):
            group = ctx_idx + 1 + lax.div(k, inner_count)
            d = lax.rem(group * inner_count + lax.rem(inner_idx + k, inner_count), n)
            copy_to(src.at[c, d, tensors], dst.at[c, me, tensors], (kind + 1, c), d).start()
            return carry

        def own(k, carry):
            d = ctx_idx * inner_count + lax.rem(inner_idx + k, inner_count)
            copy_to(src.at[c, d], dst.at[c, me], (kind, c), d).start()
            return carry

        lax.fori_loop(0, rest, cross, 0)
        lax.fori_loop(1, inner_count, own, 0)

    def spread_all(src, dst, c, kind, tensors):
        few, many = pl.ds(0, inner_count - 1), pl.ds(0, rest)
        return (
            copy_to(src.at[c, few], dst.at[c, few], (kind, c), other),
            copy_to(src.at[c, many, tensors], dst.at[c, many, tensors], (kind + 1, c), other),
        )

    shared, full = pl.ds(0, 2), pl.ds(0, 3)

    def start_in(c):
        spread(send, got, c, 0, shared)

    def all_in(c):
        return spread_all(send, got, c, 0, shared)

    def all_out(c):
        return spread_all(out, back, c, 2, full if c == chunks - 1 else shared)

    def relays(c):
        if c == chunks - 1:
            return []
        group = pl.ds(pl.multiple_of(ctx_idx * inner_count, inner_count), inner_count)
        return [
            copy_to(
                back.at[c, group, 2],
                back.at[c, group, 2],
                (3 + p, c),
                lax.rem(me + p * inner_count, n),
            )
            for p in range(1, ctx_count)
        ]

    def by_channel(block):
        return jnp.transpose(block).reshape(n, SUBLANES, width)

    for load in loads[:4]:
        load.wait()
    for c in range(chunks):
        cols = slice(c * span, (c + 1) * span)
        send[c, :, 0] = by_channel(value[:, cols])
        send[c, :, 1] = by_channel(cot[:, cols] * gate[:, cols])
        send[c, :, 2] = by_channel(taps[:, cols])
        if c == 0:
            pl.semaphore_wait(barrier, n - 1)
        start_in(c)
        got[c, me] = send[c, me]

    for load in loads[4:]:
        load.wait()
    rows = [rate[...], coeff[...], keep[...]]
    filled = sum(r.shape[0] for r in rows)
    rows.append(jnp.zeros((LANES - filled, rate.shape[1]), jnp.float32))
    params[...] = jnp.transpose(jnp.concatenate(rows, 0))
    cosine, sine = circle[:, :width], circle[:, width:]
    for high, low, sign in ((ahead_high, ahead_low, 1.0), (behind_high, behind_low, -1.0)):
        table = jnp.concatenate(
            [
                jnp.concatenate([cosine, -sign * sine], 1),
                jnp.concatenate([sign * sine, cosine], 1),
            ],
            0,
        )
        top = table.astype(jnp.bfloat16)
        high[...] = top
        low[...] = (table - top.astype(jnp.float32)).astype(jnp.bfloat16)
    spec[:, half] = jnp.zeros(spec.shape[:1] + spec.shape[2:], jnp.float32)

    lane = lax.broadcasted_iota(jnp.int32, (SUBLANES, width), 1).astype(jnp.float32)

    def per_channel(chunk):
        own = params[pl.ds(pl.multiple_of(chunk * span + me * SUBLANES, SUBLANES), SUBLANES), :]

        def wide(column):
            return jnp.broadcast_to(own[:, column : column + 1], (SUBLANES, width))

        rates = [wide(m) for m in range(modes)]
        coeffs = [wide(modes + m) for m in range(modes)]
        keeps = [
            [wide((2 + g) * modes + m) for m in range(modes)] for g in range(ctx_count - 1)
        ]
        return rates, coeffs, keeps

    def add_tail(c):
        rates, coeffs, _ = per_channel(c)
        steps = [jnp.exp(-r * float(width)) for r in rates]
        terms = [f * jnp.exp(-r * lane) for r, f in zip(rates, coeffs)]
        base = ctx_idx * inner_count
        for i in range(inner_count):
            got[c, base + i, 2] = got[c, base + i, 2] + sum(terms[1:], terms[0])
            terms = [t * s for t, s in zip(terms, steps)]

    def rows_ahead(c, base, tensor, slot):
        blank = (None, None)
        xs = [(got[c, base + i, tensor], None) for i in range(inner_count)] + [blank] * inner_count
        parts = transform_ahead(xs)
        for k in range(half):
            real, imag = parts[k]
            cosine, sine = twist[0, k : k + 1, :], twist[1, k : k + 1, :]
            if imag is None:
                first, second = real * cosine, -(real * sine)
            else:
                first, second = real * cosine + imag * sine, imag * cosine - real * sine
            spec[slot, k, :, :width] = first
            spec[slot, k, :, width:] = second

    def lines(high, low):
        data = spec[...].reshape(-1, 2 * width)
        top = data.astype(jnp.bfloat16)
        rest_part = (data - top.astype(jnp.float32)).astype(jnp.bfloat16)
        dot = functools.partial(jnp.dot, preferred_element_type=jnp.float32)
        result = dot(rest_part, high[...]) + dot(top, low[...]) + dot(top, high[...])
        spec[...] = result.reshape(spec.shape)

    def rows_behind(slot):
        xs = []
        for k in range(half):
            real, imag = spec[slot, k, :, :width], spec[slot, k, :, width:]
            cosine, sine = twist[2, k : k + 1, :], twist[3, k : k + 1, :]
            xs.append((real * cosine - imag * sine, real * sine + imag * cosine))
        xs += [(None, None)] * (row_count - half)
        return [y[0] for y in transform_behind(xs)[:inner_count]]

    kern_slot, value_slot, grad_slot = 0, 1, 1 + ctx_count
    grad_scale = 1.0 / math.sqrt(group_len * ctx_count)

    def multiply(k, carry):
        def load(slot):
            return spec[slot, k, :, :width], spec[slot, k, :, width:]

        def store(slot, real, imag):
            spec[slot, k, :, :width] = real
            spec[slot, k, :, width:] = imag

        kr, ki = load(kern_slot)
        corr_r = corr_i = 0.0
        for g in range(ctx_count):
            vr, vi = load(value_slot + g)
            gr, gi = load(grad_slot + g)
            corr_r = corr_r + (vr * gr + vi * gi)
            corr_i = corr_i + (vr * gi - vi * gr)
            store(value_slot + g, kr * vr - ki * vi, kr * vi + ki * vr)
            store(grad_slot + g, kr * gr + ki * gi, kr * gi - ki * gr)
        store(kern_slot, corr_r, corr_i)
        return carry

    def carried_ahead(chunk):
        rates, coeffs, keeps = per_channel(chunk)
        steps = [jnp.exp(-r * float(width)) for r in rates]
        whole = [jnp.exp(-r * float(group_len)) for r in rates]
        to_end = [jnp.exp(-r * (width - 1.0 - lane)) for r in rates]
        from_start = [c * jnp.exp(-r * (lane + 1.0)) for r, c in zip(rates, coeffs)]
        state = [jnp.zeros((SUBLANES, 1), jnp.float32)] * modes
        for g in range(ctx_count - 1):
            acc = [jnp.zeros((SUBLANES, width), jnp.float32)] * modes
            for i in range(inner_count):
                block = got[chunk, g * inner_count + i, 0]
                acc = [a * s + block for a, s in zip(acc, steps)]
            for m in range(modes):
                total = jnp.sum(acc[m] * to_end[m], 1, keepdims=True)
                state[m] = keeps[g][m][:, :1] * (whole[m][:, :1] * state[m] + total)
            terms = [f * st for f, st in zip(from_start, state)]
            for i in range(inner_count):
                row = (g + 1) * inner_count + i
                out[chunk, row, 0] = out[chunk, row, 0] + sum(terms[1:], terms[0])
                terms = [t * s for t, s in zip(terms, steps)]

    def carried_behind(chunk):
        rates, coeffs, keeps = per_channel(chunk)
        steps = [jnp.exp(-r * float(width)) for r in rates]
        whole = [jnp.exp(-r * float(group_len)) for r in rates]
        to_end = [jnp.exp(-r * (width - 1.0 - lane)) for r in rates]
        from_start = [c * jnp.exp(-r * (lane + 1.0)) for r, c in zip(rates, coeffs)]
        state = [jnp.zeros((SUBLANES, 1), jnp.float32)] * modes
        for g in reversed(range(1, ctx_count)):
            acc = [jnp.zeros((SUBLANES, width), jnp.float32)] * modes
            for i in reversed(range(inner_count)):
                block = got[chunk, g * inner_count + i, 1]
                acc = [a * s + block for a, s in zip(acc, steps)]
            for m in range(modes):
                total = jnp.sum(acc[m] * from_start[m], 1, keepdims=True)
                if g < ctx_count - 1:
                    state[m] = total + whole[m][:, :1] * keeps[g][m][:, :1] * state[m]
                else:
                    state[m] = total
            terms = [
                t * (kp[:, :1] * st) for t, kp, st in zip(to_end, keeps[g - 1], state)
            ]
            for i in reversed(range(inner_count)):
                row = (g - 1) * inner_count + i
                out[chunk, row, 1] = out[chunk, row, 1] + sum(terms[1:], terms[0])
                terms = [t * s for t, s in zip(terms, steps)]

    def process(c, carry):
        for whole in all_in(c):
            whole.wait_recv()
        add_tail(c)
        rows_ahead(c, ctx_idx * inner_count, 2, kern_slot)

        def ahead(step, inner_carry):
            tensor, g = lax.div(step, ctx_count), lax.rem(step, ctx_count)
            rows_ahead(c, g * inner_count, tensor, 1 + step)
            return inner_carry

        lax.fori_loop(0, 2 * ctx_count, ahead, 0)
        lines(ahead_high, ahead_low)
        lax.fori_loop(0, half, multiply, 0)
        lines(behind_high, behind_low)
        for i, y in enumerate(rows_behind(kern_slot)):
            y = y * grad_scale
            for g in range(ctx_count):
                out[c, g * inner_count + i, 2] = y

        def behind(step, inner_carry):
            tensor, g = lax.div(step, ctx_count), lax.rem(step, ctx_count)
            for i, y in enumerate(rows_behind(1 + step)):
                out[c, g * inner_count + i, tensor] = y
            return inner_carry

        lax.fori_loop(0, 2 * ctx_count, behind, 0)
        carried_ahead(c)
        carried_behind(c)
        back[c, me] = out[c, me]

        @pl.when(c < chunks - 1)
        def _():
            spread(out, back, c, 2, shared)

        @pl.when(c == chunks - 1)
        def _():
            spread(out, back, c, 2, full)

        return carry

    lax.fori_loop(0, chunks, process, 0)

    def by_token(c, tensor):
        return jnp.transpose(back[c, :, tensor].reshape(span, width))

    for c in range(chunks):
        if c < chunks - 1:
            all_out(c)[0].wait_recv()
        for relay in relays(c):
            relay.start()
    stores = []
    for c in range(chunks):
        cols = slice(c * span, (c + 1) * span)
        if c == chunks - 1:
            all_out(c)[0].wait_recv()
        all_out(c)[1].wait_recv()
        mixture = by_token(c, 0)
        mixed_out[:, cols] = gate[:, cols] * mixture
        grad_gate[:, cols] = cot[:, cols] * mixture
        grad_value[:, cols] = by_token(c, 1)
        for relay in relays(c):
            relay.wait_recv()
        grad_filter[:, cols] = by_token(c, 2)
        moves = (
            (mixed_out, mixed_hbm),
            (grad_gate, gated_hbm),
            (grad_value, turned_hbm),
            (grad_filter, filtered_hbm),
        )
        for i, (src, dst) in enumerate(moves):
            part = pl.ds(c * span, span)
            store = pltpu.make_async_copy(src.at[:, part], dst.at[:, part], store_sems.at[i, c])
            store.start()
            stores.append(store)
    for c in range(chunks):
        for whole in (*all_in(c), *all_out(c), *relays(c)):
            whole.wait_send()
    for store in stores:
        store.wait()


def finish_kernel(*refs):
    sources, targets, held, load_sems, store_sems = refs[:4], refs[4:8], refs[8:12], refs[12], refs[13]
    loads = [
        pltpu.make_async_copy(src, mid, load_sems.at[i])
        for i, (src, mid) in enumerate(zip(sources, held))
    ]
    stores = [
        pltpu.make_async_copy(mid, dst, store_sems.at[i])
        for i, (mid, dst) in enumerate(zip(held, targets))
    ]
    for load in loads:
        load.start()
    for load, store in zip(loads, stores):
        load.wait()
        store.start()
    for store in stores:
        store.wait()


def fits(mesh, value_input):
    inner_count, ctx_count = mesh.shape["inner"], mesh.shape["ctx"]
    tok_dev, channels = value_input.shape
    return (
        tok_dev == LANES
        and ctx_count > 1
        and channels % (inner_count * ctx_count * SUBLANES) == 0
        and inner_count & (inner_count - 1) == 0
    )


def shards_by_channel(
    mesh, gate_input, value_input, filter_taps, decay_rate, mode_coeff, boundary_keep, cotangent
):
    inner_count, ctx_count = mesh.shape["inner"], mesh.shape["ctx"]
    n = inner_count * ctx_count
    tok_dev, channels = value_input.shape
    modes = decay_rate.shape[0]
    chunks = channels // (n * SUBLANES)
    half = inner_count + 1
    tables = line_tables(tok_dev, 2 * inner_count, half)
    keep_rows = boundary_keep.reshape(-1, channels)
    block = jax.ShapeDtypeStruct((tok_dev, channels), jnp.float32)
    f32 = functools.partial(pltpu.VMEM, dtype=jnp.float32)
    pieces = f32((chunks, n, 3, SUBLANES, tok_dev))
    hbm = pl.BlockSpec(memory_space=pltpu.HBM)
    operands = (
        gate_input,
        value_input,
        filter_taps,
        decay_rate,
        mode_coeff,
        keep_rows,
        cotangent,
        *tables,
    )
    results = pl.pallas_call(
        functools.partial(mixer_kernel, ctx_count, inner_count, modes),
        out_shape=(block,) * 4,
        in_specs=[hbm] * len(operands),
        out_specs=(hbm,) * 4,
        scratch_shapes=[pltpu.VMEM(a.shape, a.dtype) for a in operands]
        + [pltpu.VMEM((2 * tok_dev, 2 * tok_dev), jnp.bfloat16)] * 4
        + [
            pieces,
            pieces,
            f32((1 + 2 * ctx_count, half + 1, SUBLANES, 2 * tok_dev)),
            f32((channels, LANES)),
            pieces,
            pieces,
        ]
        + [f32((tok_dev, channels))] * 4
        + [
            pltpu.SemaphoreType.DMA((len(operands),)),
            pltpu.SemaphoreType.DMA((4, chunks)),
            pltpu.SemaphoreType.DMA((3 + ctx_count, chunks)),
            pltpu.SemaphoreType.DMA((3 + ctx_count, chunks)),
        ],
        compiler_params=pltpu.CompilerParams(
            collective_id=0, has_side_effects=True, vmem_limit_bytes=60 * 1024 * 1024
        ),
    )(*operands)
    return pl.pallas_call(
        finish_kernel,
        out_shape=(block,) * 4,
        in_specs=[hbm] * 4,
        out_specs=(hbm,) * 4,
        scratch_shapes=[f32((tok_dev, channels))] * 4
        + [pltpu.SemaphoreType.DMA((4,)), pltpu.SemaphoreType.DMA((4,))],
        compiler_params=pltpu.CompilerParams(vmem_limit_bytes=60 * 1024 * 1024),
    )(*results)


def shards_of(mesh, *args):
    if fits(mesh, args[1]):
        return shards_by_channel(mesh, *args)
    return shards(*args)


def solution(mesh):
    placed = (
        P(("ctx", "inner"), None),
        P(("ctx", "inner"), None),
        P("inner", None),
        P(),
        P(),
        P(),
        P(("ctx", "inner"), None),
    )
    return jax.shard_map(
        functools.partial(shards_of, mesh),
        mesh=mesh,
        in_specs=placed,
        out_specs=(
            P(("ctx", "inner"), None),
            P(("ctx", "inner"), None),
            P(("ctx", "inner"), None),
            P("inner", None),
        ),
        check_vma=False,
    )
```

```python
import functools
import math

import jax
import jax.numpy as jnp
import numpy as np
from jax import lax
from jax.experimental import pallas as pl
from jax.experimental.pallas import tpu as pltpu
from jax.sharding import PartitionSpec as P

FULL_PRECISION = lax.Precision.HIGHEST


def prefix(part, axis, combine, identity, reverse):
    count = lax.axis_size(axis)
    place = lax.axis_index(axis)
    ahead = count - 1 - place if reverse else place
    gathered = jax.tree.map(lambda a: lax.all_gather(a, axis), part)
    state = jax.tree.map(lambda a, e: jnp.zeros_like(a) + jnp.asarray(e, a.dtype), part, identity)

    def one(hop, state):
        source = count - 1 - hop if reverse else hop
        return combine(
            state, jax.tree.map(lambda a: lax.dynamic_index_in_dim(a, source, 0, False), gathered)
        )

    return lax.fori_loop(0, ahead, one, state)


def turn_table(left_index, right_index, period):
    phase = (left_index * right_index % period).astype(jnp.float32) * (2.0 * math.pi / period)
    return (jnp.cos(phase), jnp.sin(phase))


def ahead_table(cosine, sine):
    return jnp.stack([jnp.stack([cosine, sine], 0), jnp.stack([-sine, cosine], 0)], 0)


def behind_table(cosine, sine):
    return jnp.stack([jnp.stack([cosine, -sine], 0), jnp.stack([sine, cosine], 0)], 0)


def contract(form, table, data):
    return jnp.einsum(form, table, data, precision=FULL_PRECISION)


def combine_links(earlier, later_link):
    return (later_link[0] * earlier[0], later_link[0] * earlier[1] + later_link[1])


def carried_mode_state(decay_factors, partial_terms, backward_pass):
    unit_links = jnp.ones_like(decay_factors)
    blank_terms = jnp.zeros_like(partial_terms)
    summed_total = lax.psum(partial_terms, "inner")
    return prefix(
        (decay_factors, summed_total),
        "ctx",
        combine_links,
        (unit_links, blank_terms),
        backward_pass,
    )[1]


def shards(gate_input, value_input, filter_taps, decay_rate, mode_coeff, boundary_keep, cotangent):
    tok_dev = value_input.shape[0]
    inner_count = lax.axis_size("inner")
    ctx_count = lax.axis_size("ctx")
    group_len = tok_dev * inner_count
    fft_len = 2 * group_len
    row_count = 2 * inner_count
    col_count = tok_dev // inner_count
    inner_idx = lax.axis_index("inner")
    ctx_idx = lax.axis_index("ctx")
    row_range = jnp.arange(row_count, dtype=jnp.int32)
    inner_range = jnp.arange(inner_count, dtype=jnp.int32)
    tok_range = jnp.arange(tok_dev, dtype=jnp.int32)
    owner_of_row = row_range // 2
    mirrored_label = jnp.where(owner_of_row == 0, inner_count, row_count - owner_of_row)
    row_label = jnp.where(row_range % 2 == 0, owner_of_row, mirrored_label)
    cos_rows, sin_rows = turn_table(row_label[:, None], inner_range[None, :], row_count)
    rows_table = ahead_table(cos_rows, sin_rows)
    col_index = inner_idx * col_count + jnp.arange(col_count, dtype=jnp.int32)
    cos_twist, sin_twist = turn_table(row_label[:, None, None], col_index[None, :, None], fft_len)
    cos_line, sin_line = turn_table(tok_range[:, None], tok_range[None, :], tok_dev)
    line_ahead = ahead_table(cos_line, sin_line)
    line_behind = behind_table(cos_line, sin_line)
    own_rows = lax.dynamic_slice_in_dim(row_label, 2 * inner_idx, 2, 0)
    cos_untwist, sin_untwist = turn_table(
        own_rows[:, None, None], tok_range[None, :, None], fft_len
    )
    cos_back, sine_reverse = turn_table(inner_range[:, None], row_label[None, :], row_count)
    back_table = behind_table(cos_back, sine_reverse)

    def to_spectrum(signals):
        stacked = jnp.stack(signals, 0)[:, None]
        columns = lax.all_to_all(stacked, "inner", split_axis=2, concat_axis=1, tiled=True)
        count = len(signals)
        parts = contract("pqki,qijc->pkjc", rows_table[:, :count], columns)
        turned = jnp.stack(
            [
                parts[0] * cos_twist + parts[1] * sin_twist,
                parts[1] * cos_twist - parts[0] * sin_twist,
            ],
            0,
        )
        spread = lax.all_to_all(turned, "inner", split_axis=1, concat_axis=2, tiled=True)
        return contract("pqkj,qbjc->pbkc", line_ahead, spread)

    def from_spectrum(spec, keep_imag):
        line = contract("pqjk,qbkc->pbjc", line_behind, spec)
        turned = jnp.stack(
            [
                line[0] * cos_untwist - line[1] * sin_untwist,
                line[1] * cos_untwist + line[0] * sin_untwist,
            ],
            0,
        )
        back = lax.all_to_all(turned, "inner", split_axis=2, concat_axis=1, tiled=True)
        count = 2 if keep_imag else 1
        row_values = contract("pqik,qkjc->pijc", back_table[:count], back) * (1.0 / fft_len)
        joined = lax.all_to_all(row_values, "inner", split_axis=1, concat_axis=2, tiled=True)
        return joined[:, 0]

    def mirror_rows(spec):
        flipped = spec[:, ::-1]
        rolled = jnp.roll(flipped, 1, axis=1)
        leading_device = jnp.stack([rolled[0], flipped[1]], 0)
        return jnp.where(inner_idx == 0, leading_device, flipped[::-1])

    def times_kernel_conj(kern, spec):
        return jnp.stack(
            [kern[0] * spec[0] + kern[1] * spec[1], kern[0] * spec[1] - kern[1] * spec[0]], 0
        )

    positions = (inner_idx * tok_dev + tok_range).astype(jnp.float32)
    rate_wide = decay_rate[:, None, :]
    coeff_wide = mode_coeff[:, None, :]
    to_end_pow = jnp.exp(-rate_wide * (group_len - 1.0 - positions)[None, :, None])
    from_start_pow = coeff_wide * jnp.exp(-rate_wide * (positions + 1.0)[None, :, None])
    tail_part = jnp.sum(coeff_wide * jnp.exp(-rate_wide * positions[None, :, None]), 0)
    group_decay = jnp.exp(-decay_rate * float(group_len))
    keep_full = jnp.concatenate(
        [boundary_keep, jnp.ones((1,) + boundary_keep.shape[1:], jnp.float32)], 0
    )
    keep_row = lax.dynamic_index_in_dim(keep_full, ctx_idx, 0, keepdims=False)
    link_decay = keep_row * group_decay
    kernel = filter_taps + tail_part
    kern_spec = to_spectrum((kernel,))
    mix_grad = cotangent * gate_input
    packed = to_spectrum((value_input, mix_grad))
    mirror_real = mirror_rows(packed[0])
    mirror_imag = mirror_rows(packed[1])
    val_spec = jnp.stack([0.5 * (packed[0] + mirror_real), 0.5 * (packed[1] - mirror_imag)], 0)
    grad_spec = jnp.stack([0.5 * (packed[1] + mirror_imag), 0.5 * (mirror_real - packed[0])], 0)
    ahead = jnp.stack(
        [
            kern_spec[0] * val_spec[0] - kern_spec[1] * val_spec[1],
            kern_spec[0] * val_spec[1] + kern_spec[1] * val_spec[0],
        ],
        0,
    )
    behind = times_kernel_conj(kern_spec, grad_spec)
    both_parts = from_spectrum(jnp.stack([ahead[0] - behind[1], ahead[1] + behind[0]], 0), True)
    inside = both_parts[0]
    through = both_parts[1]
    local_sums = jnp.sum(to_end_pow * value_input[None], 1)
    starts = carried_mode_state(link_decay, keep_row * local_sums, False)
    mixture = inside + jnp.sum(from_start_pow * starts[:, None, :], 0)
    mixed_out = gate_input * mixture
    grad_gate = cotangent * mixture
    pull_terms = jnp.sum(from_start_pow * mix_grad[None], 1)
    later_state = carried_mode_state(link_decay, pull_terms, True)
    grad_value = through + jnp.sum(to_end_pow * (keep_row * later_state)[:, None, :], 0)
    corr = times_kernel_conj(val_spec, grad_spec)
    share_spec = lax.psum_scatter(corr, "ctx", scatter_dimension=3, tiled=True)
    share_grad = from_spectrum(share_spec, False)[0]
    grad_filter = lax.all_gather(share_grad, "ctx", axis=1, tiled=True)
    grad_scale = 1.0 / math.sqrt(group_len * ctx_count)
    return (mixed_out, grad_gate, grad_value, grad_filter * grad_scale)


LANES = 128
SUBLANES = 8


def plus(x, y):
    return tuple(q if p is None else p if q is None else p + q for p, q in zip(x, y))


def minus(x, y):
    return tuple(
        p if q is None else -q if p is None else p - q for p, q in zip(x, y)
    )


def scaled(part, factor):
    if part is None or abs(factor) < 1e-12:
        return None
    if abs(factor - 1.0) < 1e-12:
        return part
    if abs(factor + 1.0) < 1e-12:
        return -part
    return part * factor


def turned(x, angle):
    c, s = math.cos(angle), math.sin(angle)
    real = minus((scaled(x[0], c),), (scaled(x[1], s),))[0] if x[1] is not None else scaled(x[0], c)
    imag = plus((scaled(x[0], s),), (scaled(x[1], c),))[0]
    return (real, imag)


def transform_ahead(xs):
    n = len(xs)
    if n == 1:
        return xs
    h = n // 2
    total = [plus(xs[i], xs[i + h]) for i in range(h)]
    apart = [turned(minus(xs[i], xs[i + h]), -2.0 * math.pi * i / n) for i in range(h)]
    even, odd = transform_ahead(total), transform_ahead(apart)
    return [(even, odd)[k % 2][k // 2] for k in range(n)]


def transform_behind(xs):
    n = len(xs)
    if n == 1:
        return xs
    h = n // 2
    even, odd = transform_behind(xs[0::2]), transform_behind(xs[1::2])
    odd = [turned(odd[i], 2.0 * math.pi * i / n) for i in range(h)]
    return [plus(even[i], odd[i]) for i in range(h)] + [minus(even[i], odd[i]) for i in range(h)]


def line_tables(width, row_count, half):
    turn = 2.0 * np.pi / width * (np.outer(np.arange(width), np.arange(width)) % width)
    c, s = np.cos(turn), np.sin(turn)
    line = np.concatenate([c, s], 1).astype(np.float32)
    length = width * row_count
    phase = 2.0 * np.pi / length * np.outer(np.arange(half), np.arange(width))
    weight = np.full((half, 1), 2.0)
    weight[0] = weight[-1] = 1.0
    twist = np.stack(
        [np.cos(phase), np.sin(phase), np.cos(phase) * weight / length, np.sin(phase) * weight / length]
    ).astype(np.float32)
    return line, twist


def mixer_kernel(
    ctx_count,
    inner_count,
    modes,
    gate_hbm,
    value_hbm,
    taps_hbm,
    rate_hbm,
    coeff_hbm,
    keep_hbm,
    cot_hbm,
    circle_hbm,
    twist_hbm,
    mixed_hbm,
    gated_hbm,
    turned_hbm,
    filtered_hbm,
    gate,
    value,
    taps,
    rate,
    coeff,
    keep,
    cot,
    circle,
    twist,
    ahead_high,
    ahead_low,
    behind_high,
    behind_low,
    send,
    got,
    spec,
    params,
    out,
    back,
    mixed_out,
    grad_gate,
    grad_value,
    grad_filter,
    load_sems,
    store_sems,
    send_sems,
    recv_sems,
):
    n = ctx_count * inner_count
    width = value.shape[0]
    chunks = send.shape[0]
    span = n * SUBLANES
    row_count = 2 * inner_count
    half = inner_count + 1
    group_len = width * inner_count
    ctx_idx = lax.axis_index("ctx")
    inner_idx = lax.axis_index("inner")
    me = ctx_idx * inner_count + inner_idx

    pairs = (
        (taps_hbm, taps),
        (value_hbm, value),
        (gate_hbm, gate),
        (cot_hbm, cot),
        (rate_hbm, rate),
        (coeff_hbm, coeff),
        (keep_hbm, keep),
        (twist_hbm, twist),
        (circle_hbm, circle),
    )
    loads = [
        pltpu.make_async_copy(src, dst, load_sems.at[i]) for i, (src, dst) in enumerate(pairs)
    ]
    for load in loads:
        load.start()

    barrier = pltpu.get_barrier_semaphore()

    def greet(k, carry):
        d = lax.rem(me + k, n)
        pl.semaphore_signal(
            barrier,
            inc=1,
            device_id=(lax.div(d, inner_count), lax.rem(d, inner_count)),
            device_id_type=pl.DeviceIdType.MESH,
        )
        return carry

    lax.fori_loop(1, n, greet, 0)

    def copy_to(src, dst, kind, d):
        return pltpu.make_async_remote_copy(
            src_ref=src,
            dst_ref=dst,
            send_sem=send_sems.at[kind[0], kind[1]],
            recv_sem=recv_sems.at[kind[0], kind[1]],
            device_id=(lax.div(d, inner_count), lax.rem(d, inner_count)),
            device_id_type=pl.DeviceIdType.MESH,
        )

    rest = n - inner_count
    other = lax.rem(me + 1, n)

    def spread(src, dst, c, kind, tensors):
        def cross(k, carry):
            group = ctx_idx + 1 + lax.div(k, inner_count)
            place = lax.rem(inner_idx + inner_count // 2 + k, inner_count)
            d = lax.rem(group * inner_count + place, n)
            copy_to(src.at[c, d, tensors], dst.at[c, me, tensors], (kind + 1, c), d).start()
            return carry

        def own(k, carry):
            shift = 1 + lax.rem(k + inner_count // 2 - 2, inner_count - 1)
            d = ctx_idx * inner_count + lax.rem(inner_idx + shift, inner_count)
            copy_to(src.at[c, d], dst.at[c, me], (kind, c), d).start()
            return carry

        lax.fori_loop(0, rest, cross, 0)
        lax.fori_loop(1, inner_count, own, 0)

    def spread_all(src, dst, c, kind, tensors):
        few, many = pl.ds(0, inner_count - 1), pl.ds(0, rest)
        return (
            copy_to(src.at[c, few], dst.at[c, few], (kind, c), other),
            copy_to(src.at[c, many, tensors], dst.at[c, many, tensors], (kind + 1, c), other),
        )

    shared, full = pl.ds(0, 2), pl.ds(0, 3)

    def start_in(c):
        spread(send, got, c, 0, shared)

    def all_in(c):
        return spread_all(send, got, c, 0, shared)

    def all_out(c):
        return spread_all(out, back, c, 2, full if c == chunks - 1 else shared)

    def relays(c):
        if c == chunks - 1:
            return []
        group = pl.ds(pl.multiple_of(ctx_idx * inner_count, inner_count), inner_count)
        return [
            copy_to(
                back.at[c, group, 2],
                back.at[c, group, 2],
                (3 + p, c),
                lax.rem(me + p * inner_count, n),
            )
            for p in range(1, ctx_count)
        ]

    def by_channel(block):
        return jnp.transpose(block).reshape(n, SUBLANES, width)

    for load in loads[:4]:
        load.wait()
    for c in range(chunks):
        cols = slice(c * span, (c + 1) * span)
        send[c, :, 0] = by_channel(value[:, cols])
        send[c, :, 1] = by_channel(cot[:, cols] * gate[:, cols])
        send[c, :, 2] = by_channel(taps[:, cols])
        if c == 0:
            pl.semaphore_wait(barrier, n - 1)
        start_in(c)
        got[c, me] = send[c, me]

    for load in loads[4:]:
        load.wait()
    rows = [rate[...], coeff[...], keep[...]]
    filled = sum(r.shape[0] for r in rows)
    rows.append(jnp.zeros((LANES - filled, rate.shape[1]), jnp.float32))
    params[...] = jnp.transpose(jnp.concatenate(rows, 0))
    cosine, sine = circle[:, :width], circle[:, width:]
    for high, low, sign in ((ahead_high, ahead_low, 1.0), (behind_high, behind_low, -1.0)):
        table = jnp.concatenate(
            [
                jnp.concatenate([cosine, -sign * sine], 1),
                jnp.concatenate([sign * sine, cosine], 1),
            ],
            0,
        )
        top = table.astype(jnp.bfloat16)
        high[...] = top
        low[...] = (table - top.astype(jnp.float32)).astype(jnp.bfloat16)
    spec[:, half] = jnp.zeros(spec.shape[:1] + spec.shape[2:], jnp.float32)

    lane = lax.broadcasted_iota(jnp.int32, (SUBLANES, width), 1).astype(jnp.float32)

    def per_channel(chunk):
        own = params[pl.ds(pl.multiple_of(chunk * span + me * SUBLANES, SUBLANES), SUBLANES), :]

        def wide(column):
            return jnp.broadcast_to(own[:, column : column + 1], (SUBLANES, width))

        rates = [wide(m) for m in range(modes)]
        coeffs = [wide(modes + m) for m in range(modes)]
        keeps = [
            [wide((2 + g) * modes + m) for m in range(modes)] for g in range(ctx_count - 1)
        ]
        return rates, coeffs, keeps

    def add_tail(c):
        rates, coeffs, _ = per_channel(c)
        steps = [jnp.exp(-r * float(width)) for r in rates]
        terms = [f * jnp.exp(-r * lane) for r, f in zip(rates, coeffs)]
        base = ctx_idx * inner_count
        for i in range(inner_count):
            got[c, base + i, 2] = got[c, base + i, 2] + sum(terms[1:], terms[0])
            terms = [t * s for t, s in zip(terms, steps)]

    def rows_ahead(c, base, tensor, slot):
        blank = (None, None)
        xs = [(got[c, base + i, tensor], None) for i in range(inner_count)] + [blank] * inner_count
        parts = transform_ahead(xs)
        for k in range(half):
            real, imag = parts[k]
            cosine, sine = twist[0, k : k + 1, :], twist[1, k : k + 1, :]
            if imag is None:
                first, second = real * cosine, -(real * sine)
            else:
                first, second = real * cosine + imag * sine, imag * cosine - real * sine
            spec[slot, k, :, :width] = first
            spec[slot, k, :, width:] = second

    def lines(high, low):
        data = spec[...].reshape(-1, 2 * width)
        top = data.astype(jnp.bfloat16)
        rest_part = (data - top.astype(jnp.float32)).astype(jnp.bfloat16)
        dot = functools.partial(jnp.dot, preferred_element_type=jnp.float32)
        result = dot(rest_part, high[...]) + dot(top, low[...]) + dot(top, high[...])
        spec[...] = result.reshape(spec.shape)

    def rows_behind(slot):
        xs = []
        for k in range(half):
            real, imag = spec[slot, k, :, :width], spec[slot, k, :, width:]
            cosine, sine = twist[2, k : k + 1, :], twist[3, k : k + 1, :]
            xs.append((real * cosine - imag * sine, real * sine + imag * cosine))
        xs += [(None, None)] * (row_count - half)
        return [y[0] for y in transform_behind(xs)[:inner_count]]

    kern_slot, value_slot, grad_slot = 0, 1, 1 + ctx_count
    grad_scale = 1.0 / math.sqrt(group_len * ctx_count)

    def multiply(k, carry):
        def load(slot):
            return spec[slot, k, :, :width], spec[slot, k, :, width:]

        def store(slot, real, imag):
            spec[slot, k, :, :width] = real
            spec[slot, k, :, width:] = imag

        kr, ki = load(kern_slot)
        corr_r = corr_i = 0.0
        for g in range(ctx_count):
            vr, vi = load(value_slot + g)
            gr, gi = load(grad_slot + g)
            corr_r = corr_r + (vr * gr + vi * gi)
            corr_i = corr_i + (vr * gi - vi * gr)
            store(value_slot + g, kr * vr - ki * vi, kr * vi + ki * vr)
            store(grad_slot + g, kr * gr + ki * gi, kr * gi - ki * gr)
        store(kern_slot, corr_r, corr_i)
        return carry

    def carried_ahead(chunk):
        rates, coeffs, keeps = per_channel(chunk)
        steps = [jnp.exp(-r * float(width)) for r in rates]
        whole = [jnp.exp(-r * float(group_len)) for r in rates]
        to_end = [jnp.exp(-r * (width - 1.0 - lane)) for r in rates]
        from_start = [c * jnp.exp(-r * (lane + 1.0)) for r, c in zip(rates, coeffs)]
        state = [jnp.zeros((SUBLANES, 1), jnp.float32)] * modes
        for g in range(ctx_count - 1):
            acc = [jnp.zeros((SUBLANES, width), jnp.float32)] * modes
            for i in range(inner_count):
                block = got[chunk, g * inner_count + i, 0]
                acc = [a * s + block for a, s in zip(acc, steps)]
            for m in range(modes):
                total = jnp.sum(acc[m] * to_end[m], 1, keepdims=True)
                state[m] = keeps[g][m][:, :1] * (whole[m][:, :1] * state[m] + total)
            terms = [f * st for f, st in zip(from_start, state)]
            for i in range(inner_count):
                row = (g + 1) * inner_count + i
                out[chunk, row, 0] = out[chunk, row, 0] + sum(terms[1:], terms[0])
                terms = [t * s for t, s in zip(terms, steps)]

    def carried_behind(chunk):
        rates, coeffs, keeps = per_channel(chunk)
        steps = [jnp.exp(-r * float(width)) for r in rates]
        whole = [jnp.exp(-r * float(group_len)) for r in rates]
        to_end = [jnp.exp(-r * (width - 1.0 - lane)) for r in rates]
        from_start = [c * jnp.exp(-r * (lane + 1.0)) for r, c in zip(rates, coeffs)]
        state = [jnp.zeros((SUBLANES, 1), jnp.float32)] * modes
        for g in reversed(range(1, ctx_count)):
            acc = [jnp.zeros((SUBLANES, width), jnp.float32)] * modes
            for i in reversed(range(inner_count)):
                block = got[chunk, g * inner_count + i, 1]
                acc = [a * s + block for a, s in zip(acc, steps)]
            for m in range(modes):
                total = jnp.sum(acc[m] * from_start[m], 1, keepdims=True)
                if g < ctx_count - 1:
                    state[m] = total + whole[m][:, :1] * keeps[g][m][:, :1] * state[m]
                else:
                    state[m] = total
            terms = [
                t * (kp[:, :1] * st) for t, kp, st in zip(to_end, keeps[g - 1], state)
            ]
            for i in reversed(range(inner_count)):
                row = (g - 1) * inner_count + i
                out[chunk, row, 1] = out[chunk, row, 1] + sum(terms[1:], terms[0])
                terms = [t * s for t, s in zip(terms, steps)]

    def process(c, carry):
        for whole in all_in(c):
            whole.wait_recv()
        add_tail(c)
        rows_ahead(c, ctx_idx * inner_count, 2, kern_slot)

        def ahead(step, inner_carry):
            tensor, g = lax.div(step, ctx_count), lax.rem(step, ctx_count)
            rows_ahead(c, g * inner_count, tensor, 1 + step)
            return inner_carry

        lax.fori_loop(0, 2 * ctx_count, ahead, 0)
        lines(ahead_high, ahead_low)
        lax.fori_loop(0, half, multiply, 0)
        lines(behind_high, behind_low)
        for i, y in enumerate(rows_behind(kern_slot)):
            y = y * grad_scale
            for g in range(ctx_count):
                out[c, g * inner_count + i, 2] = y

        def behind(step, inner_carry):
            tensor, g = lax.div(step, ctx_count), lax.rem(step, ctx_count)
            for i, y in enumerate(rows_behind(1 + step)):
                out[c, g * inner_count + i, tensor] = y
            return inner_carry

        lax.fori_loop(0, 2 * ctx_count, behind, 0)
        carried_ahead(c)
        carried_behind(c)
        back[c, me] = out[c, me]

        @pl.when(c < chunks - 1)
        def _():
            spread(out, back, c, 2, shared)

        @pl.when(c == chunks - 1)
        def _():
            spread(out, back, c, 2, full)

        return carry

    lax.fori_loop(0, chunks, process, 0)

    def by_token(c, tensor):
        return jnp.transpose(back[c, :, tensor].reshape(span, width))

    for c in range(chunks):
        if c < chunks - 1:
            all_out(c)[0].wait_recv()
        for relay in relays(c):
            relay.start()
    stores = []
    for c in range(chunks):
        cols = slice(c * span, (c + 1) * span)
        if c == chunks - 1:
            all_out(c)[0].wait_recv()
        all_out(c)[1].wait_recv()
        mixture = by_token(c, 0)
        mixed_out[:, cols] = gate[:, cols] * mixture
        grad_gate[:, cols] = cot[:, cols] * mixture
        grad_value[:, cols] = by_token(c, 1)
        for relay in relays(c):
            relay.wait_recv()
        grad_filter[:, cols] = by_token(c, 2)
        moves = (
            (mixed_out, mixed_hbm),
            (grad_gate, gated_hbm),
            (grad_value, turned_hbm),
            (grad_filter, filtered_hbm),
        )
        for i, (src, dst) in enumerate(moves):
            part = pl.ds(c * span, span)
            store = pltpu.make_async_copy(src.at[:, part], dst.at[:, part], store_sems.at[i, c])
            store.start()
            stores.append(store)
    for c in range(chunks):
        for whole in (*all_in(c), *all_out(c), *relays(c)):
            whole.wait_send()
    for store in stores:
        store.wait()


def finish_kernel(*refs):
    sources, targets, held, load_sems, store_sems = refs[:4], refs[4:8], refs[8:12], refs[12], refs[13]
    loads = [
        pltpu.make_async_copy(src, mid, load_sems.at[i])
        for i, (src, mid) in enumerate(zip(sources, held))
    ]
    stores = [
        pltpu.make_async_copy(mid, dst, store_sems.at[i])
        for i, (mid, dst) in enumerate(zip(held, targets))
    ]
    for load in loads:
        load.start()
    for load, store in zip(loads, stores):
        load.wait()
        store.start()
    for store in stores:
        store.wait()


def fits(mesh, value_input):
    inner_count, ctx_count = mesh.shape["inner"], mesh.shape["ctx"]
    tok_dev, channels = value_input.shape
    return (
        tok_dev == LANES
        and ctx_count > 1
        and channels % (inner_count * ctx_count * SUBLANES) == 0
        and inner_count & (inner_count - 1) == 0
    )


def shards_by_channel(
    mesh, gate_input, value_input, filter_taps, decay_rate, mode_coeff, boundary_keep, cotangent
):
    inner_count, ctx_count = mesh.shape["inner"], mesh.shape["ctx"]
    n = inner_count * ctx_count
    tok_dev, channels = value_input.shape
    modes = decay_rate.shape[0]
    chunks = channels // (n * SUBLANES)
    half = inner_count + 1
    tables = line_tables(tok_dev, 2 * inner_count, half)
    keep_rows = boundary_keep.reshape(-1, channels)
    block = jax.ShapeDtypeStruct((tok_dev, channels), jnp.float32)
    f32 = functools.partial(pltpu.VMEM, dtype=jnp.float32)
    pieces = f32((chunks, n, 3, SUBLANES, tok_dev))
    hbm = pl.BlockSpec(memory_space=pltpu.HBM)
    operands = (
        gate_input,
        value_input,
        filter_taps,
        decay_rate,
        mode_coeff,
        keep_rows,
        cotangent,
        *tables,
    )
    results = pl.pallas_call(
        functools.partial(mixer_kernel, ctx_count, inner_count, modes),
        out_shape=(block,) * 4,
        in_specs=[hbm] * len(operands),
        out_specs=(hbm,) * 4,
        scratch_shapes=[pltpu.VMEM(a.shape, a.dtype) for a in operands]
        + [pltpu.VMEM((2 * tok_dev, 2 * tok_dev), jnp.bfloat16)] * 4
        + [
            pieces,
            pieces,
            f32((1 + 2 * ctx_count, half + 1, SUBLANES, 2 * tok_dev)),
            f32((channels, LANES)),
            pieces,
            pieces,
        ]
        + [f32((tok_dev, channels))] * 4
        + [
            pltpu.SemaphoreType.DMA((len(operands),)),
            pltpu.SemaphoreType.DMA((4, chunks)),
            pltpu.SemaphoreType.DMA((3 + ctx_count, chunks)),
            pltpu.SemaphoreType.DMA((3 + ctx_count, chunks)),
        ],
        compiler_params=pltpu.CompilerParams(
            collective_id=0, has_side_effects=True, vmem_limit_bytes=60 * 1024 * 1024
        ),
    )(*operands)
    return pl.pallas_call(
        finish_kernel,
        out_shape=(block,) * 4,
        in_specs=[hbm] * 4,
        out_specs=(hbm,) * 4,
        scratch_shapes=[f32((tok_dev, channels))] * 4
        + [pltpu.SemaphoreType.DMA((4,)), pltpu.SemaphoreType.DMA((4,))],
        compiler_params=pltpu.CompilerParams(vmem_limit_bytes=60 * 1024 * 1024),
    )(*results)


def shards_of(mesh, *args):
    if fits(mesh, args[1]):
        return shards_by_channel(mesh, *args)
    return shards(*args)


def solution(mesh):
    placed = (
        P(("ctx", "inner"), None),
        P(("ctx", "inner"), None),
        P("inner", None),
        P(),
        P(),
        P(),
        P(("ctx", "inner"), None),
    )
    return jax.shard_map(
        functools.partial(shards_of, mesh),
        mesh=mesh,
        in_specs=placed,
        out_specs=(
            P(("ctx", "inner"), None),
            P(("ctx", "inner"), None),
            P(("ctx", "inner"), None),
            P("inner", None),
        ),
        check_vma=False,
    )
```

```python
import functools
import math

import jax
import jax.numpy as jnp
import numpy as np
from jax import lax
from jax.experimental import pallas as pl
from jax.experimental.pallas import tpu as pltpu
from jax.sharding import PartitionSpec as P

FULL_PRECISION = lax.Precision.HIGHEST


def prefix(part, axis, combine, identity, reverse):
    count = lax.axis_size(axis)
    place = lax.axis_index(axis)
    ahead = count - 1 - place if reverse else place
    gathered = jax.tree.map(lambda a: lax.all_gather(a, axis), part)
    state = jax.tree.map(lambda a, e: jnp.zeros_like(a) + jnp.asarray(e, a.dtype), part, identity)

    def one(hop, state):
        source = count - 1 - hop if reverse else hop
        return combine(
            state, jax.tree.map(lambda a: lax.dynamic_index_in_dim(a, source, 0, False), gathered)
        )

    return lax.fori_loop(0, ahead, one, state)


def turn_table(left_index, right_index, period):
    phase = (left_index * right_index % period).astype(jnp.float32) * (2.0 * math.pi / period)
    return (jnp.cos(phase), jnp.sin(phase))


def ahead_table(cosine, sine):
    return jnp.stack([jnp.stack([cosine, sine], 0), jnp.stack([-sine, cosine], 0)], 0)


def behind_table(cosine, sine):
    return jnp.stack([jnp.stack([cosine, -sine], 0), jnp.stack([sine, cosine], 0)], 0)


def contract(form, table, data):
    return jnp.einsum(form, table, data, precision=FULL_PRECISION)


def combine_links(earlier, later_link):
    return (later_link[0] * earlier[0], later_link[0] * earlier[1] + later_link[1])


def carried_mode_state(decay_factors, partial_terms, backward_pass):
    unit_links = jnp.ones_like(decay_factors)
    blank_terms = jnp.zeros_like(partial_terms)
    summed_total = lax.psum(partial_terms, "inner")
    return prefix(
        (decay_factors, summed_total),
        "ctx",
        combine_links,
        (unit_links, blank_terms),
        backward_pass,
    )[1]


def shards(gate_input, value_input, filter_taps, decay_rate, mode_coeff, boundary_keep, cotangent):
    tok_dev = value_input.shape[0]
    inner_count = lax.axis_size("inner")
    ctx_count = lax.axis_size("ctx")
    group_len = tok_dev * inner_count
    fft_len = 2 * group_len
    row_count = 2 * inner_count
    col_count = tok_dev // inner_count
    inner_idx = lax.axis_index("inner")
    ctx_idx = lax.axis_index("ctx")
    row_range = jnp.arange(row_count, dtype=jnp.int32)
    inner_range = jnp.arange(inner_count, dtype=jnp.int32)
    tok_range = jnp.arange(tok_dev, dtype=jnp.int32)
    owner_of_row = row_range // 2
    mirrored_label = jnp.where(owner_of_row == 0, inner_count, row_count - owner_of_row)
    row_label = jnp.where(row_range % 2 == 0, owner_of_row, mirrored_label)
    cos_rows, sin_rows = turn_table(row_label[:, None], inner_range[None, :], row_count)
    rows_table = ahead_table(cos_rows, sin_rows)
    col_index = inner_idx * col_count + jnp.arange(col_count, dtype=jnp.int32)
    cos_twist, sin_twist = turn_table(row_label[:, None, None], col_index[None, :, None], fft_len)
    cos_line, sin_line = turn_table(tok_range[:, None], tok_range[None, :], tok_dev)
    line_ahead = ahead_table(cos_line, sin_line)
    line_behind = behind_table(cos_line, sin_line)
    own_rows = lax.dynamic_slice_in_dim(row_label, 2 * inner_idx, 2, 0)
    cos_untwist, sin_untwist = turn_table(
        own_rows[:, None, None], tok_range[None, :, None], fft_len
    )
    cos_back, sine_reverse = turn_table(inner_range[:, None], row_label[None, :], row_count)
    back_table = behind_table(cos_back, sine_reverse)

    def to_spectrum(signals):
        stacked = jnp.stack(signals, 0)[:, None]
        columns = lax.all_to_all(stacked, "inner", split_axis=2, concat_axis=1, tiled=True)
        count = len(signals)
        parts = contract("pqki,qijc->pkjc", rows_table[:, :count], columns)
        turned = jnp.stack(
            [
                parts[0] * cos_twist + parts[1] * sin_twist,
                parts[1] * cos_twist - parts[0] * sin_twist,
            ],
            0,
        )
        spread = lax.all_to_all(turned, "inner", split_axis=1, concat_axis=2, tiled=True)
        return contract("pqkj,qbjc->pbkc", line_ahead, spread)

    def from_spectrum(spec, keep_imag):
        line = contract("pqjk,qbkc->pbjc", line_behind, spec)
        turned = jnp.stack(
            [
                line[0] * cos_untwist - line[1] * sin_untwist,
                line[1] * cos_untwist + line[0] * sin_untwist,
            ],
            0,
        )
        back = lax.all_to_all(turned, "inner", split_axis=2, concat_axis=1, tiled=True)
        count = 2 if keep_imag else 1
        row_values = contract("pqik,qkjc->pijc", back_table[:count], back) * (1.0 / fft_len)
        joined = lax.all_to_all(row_values, "inner", split_axis=1, concat_axis=2, tiled=True)
        return joined[:, 0]

    def mirror_rows(spec):
        flipped = spec[:, ::-1]
        rolled = jnp.roll(flipped, 1, axis=1)
        leading_device = jnp.stack([rolled[0], flipped[1]], 0)
        return jnp.where(inner_idx == 0, leading_device, flipped[::-1])

    def times_kernel_conj(kern, spec):
        return jnp.stack(
            [kern[0] * spec[0] + kern[1] * spec[1], kern[0] * spec[1] - kern[1] * spec[0]], 0
        )

    positions = (inner_idx * tok_dev + tok_range).astype(jnp.float32)
    rate_wide = decay_rate[:, None, :]
    coeff_wide = mode_coeff[:, None, :]
    to_end_pow = jnp.exp(-rate_wide * (group_len - 1.0 - positions)[None, :, None])
    from_start_pow = coeff_wide * jnp.exp(-rate_wide * (positions + 1.0)[None, :, None])
    tail_part = jnp.sum(coeff_wide * jnp.exp(-rate_wide * positions[None, :, None]), 0)
    group_decay = jnp.exp(-decay_rate * float(group_len))
    keep_full = jnp.concatenate(
        [boundary_keep, jnp.ones((1,) + boundary_keep.shape[1:], jnp.float32)], 0
    )
    keep_row = lax.dynamic_index_in_dim(keep_full, ctx_idx, 0, keepdims=False)
    link_decay = keep_row * group_decay
    kernel = filter_taps + tail_part
    kern_spec = to_spectrum((kernel,))
    mix_grad = cotangent * gate_input
    packed = to_spectrum((value_input, mix_grad))
    mirror_real = mirror_rows(packed[0])
    mirror_imag = mirror_rows(packed[1])
    val_spec = jnp.stack([0.5 * (packed[0] + mirror_real), 0.5 * (packed[1] - mirror_imag)], 0)
    grad_spec = jnp.stack([0.5 * (packed[1] + mirror_imag), 0.5 * (mirror_real - packed[0])], 0)
    ahead = jnp.stack(
        [
            kern_spec[0] * val_spec[0] - kern_spec[1] * val_spec[1],
            kern_spec[0] * val_spec[1] + kern_spec[1] * val_spec[0],
        ],
        0,
    )
    behind = times_kernel_conj(kern_spec, grad_spec)
    both_parts = from_spectrum(jnp.stack([ahead[0] - behind[1], ahead[1] + behind[0]], 0), True)
    inside = both_parts[0]
    through = both_parts[1]
    local_sums = jnp.sum(to_end_pow * value_input[None], 1)
    starts = carried_mode_state(link_decay, keep_row * local_sums, False)
    mixture = inside + jnp.sum(from_start_pow * starts[:, None, :], 0)
    mixed_out = gate_input * mixture
    grad_gate = cotangent * mixture
    pull_terms = jnp.sum(from_start_pow * mix_grad[None], 1)
    later_state = carried_mode_state(link_decay, pull_terms, True)
    grad_value = through + jnp.sum(to_end_pow * (keep_row * later_state)[:, None, :], 0)
    corr = times_kernel_conj(val_spec, grad_spec)
    share_spec = lax.psum_scatter(corr, "ctx", scatter_dimension=3, tiled=True)
    share_grad = from_spectrum(share_spec, False)[0]
    grad_filter = lax.all_gather(share_grad, "ctx", axis=1, tiled=True)
    grad_scale = 1.0 / math.sqrt(group_len * ctx_count)
    return (mixed_out, grad_gate, grad_value, grad_filter * grad_scale)


LANES = 128
SUBLANES = 8


def plus(x, y):
    return tuple(q if p is None else p if q is None else p + q for p, q in zip(x, y))


def minus(x, y):
    return tuple(
        p if q is None else -q if p is None else p - q for p, q in zip(x, y)
    )


def scaled(part, factor):
    if part is None or abs(factor) < 1e-12:
        return None
    if abs(factor - 1.0) < 1e-12:
        return part
    if abs(factor + 1.0) < 1e-12:
        return -part
    return part * factor


def turned(x, angle):
    c, s = math.cos(angle), math.sin(angle)
    real = minus((scaled(x[0], c),), (scaled(x[1], s),))[0] if x[1] is not None else scaled(x[0], c)
    imag = plus((scaled(x[0], s),), (scaled(x[1], c),))[0]
    return (real, imag)


def transform_ahead(xs):
    n = len(xs)
    if n == 1:
        return xs
    h = n // 2
    total = [plus(xs[i], xs[i + h]) for i in range(h)]
    apart = [turned(minus(xs[i], xs[i + h]), -2.0 * math.pi * i / n) for i in range(h)]
    even, odd = transform_ahead(total), transform_ahead(apart)
    return [(even, odd)[k % 2][k // 2] for k in range(n)]


def transform_behind(xs):
    n = len(xs)
    if n == 1:
        return xs
    h = n // 2
    even, odd = transform_behind(xs[0::2]), transform_behind(xs[1::2])
    odd = [turned(odd[i], 2.0 * math.pi * i / n) for i in range(h)]
    return [plus(even[i], odd[i]) for i in range(h)] + [minus(even[i], odd[i]) for i in range(h)]


def line_tables(width, row_count, half):
    turn = 2.0 * np.pi / width * (np.outer(np.arange(width), np.arange(width)) % width)
    c, s = np.cos(turn), np.sin(turn)
    line = np.concatenate([c, s], 1).astype(np.float32)
    length = width * row_count
    phase = 2.0 * np.pi / length * np.outer(np.arange(half), np.arange(width))
    weight = np.full((half, 1), 2.0)
    weight[0] = weight[-1] = 1.0
    twist = np.stack(
        [np.cos(phase), np.sin(phase), np.cos(phase) * weight / length, np.sin(phase) * weight / length]
    ).astype(np.float32)
    return line, twist


def mixer_kernel(
    ctx_count,
    inner_count,
    modes,
    gate_hbm,
    value_hbm,
    taps_hbm,
    rate_hbm,
    coeff_hbm,
    keep_hbm,
    cot_hbm,
    circle_hbm,
    twist_hbm,
    mixed_hbm,
    gated_hbm,
    turned_hbm,
    filtered_hbm,
    gate,
    value,
    taps,
    rate,
    coeff,
    keep,
    cot,
    circle,
    twist,
    ahead_high,
    ahead_low,
    behind_high,
    behind_low,
    send,
    got,
    spec,
    params,
    out,
    back,
    mixed_out,
    grad_gate,
    grad_value,
    grad_filter,
    block_sems,
    load_sems,
    store_sems,
    send_sems,
    recv_sems,
):
    n = ctx_count * inner_count
    width = value.shape[0]
    chunks = send.shape[0]
    span = n * SUBLANES
    row_count = 2 * inner_count
    half = inner_count + 1
    group_len = width * inner_count
    ctx_idx = lax.axis_index("ctx")
    inner_idx = lax.axis_index("inner")
    me = ctx_idx * inner_count + inner_idx

    blocks = ((taps_hbm, taps), (value_hbm, value), (gate_hbm, gate), (cot_hbm, cot))
    block_loads = [
        [
            pltpu.make_async_copy(
                src.at[:, pl.ds(c * span, span)], dst.at[:, pl.ds(c * span, span)], block_sems.at[i, c]
            )
            for i, (src, dst) in enumerate(blocks)
        ]
        for c in range(chunks)
    ]
    pairs = (
        (rate_hbm, rate),
        (coeff_hbm, coeff),
        (keep_hbm, keep),
        (twist_hbm, twist),
        (circle_hbm, circle),
    )
    loads = [
        pltpu.make_async_copy(src, dst, load_sems.at[i]) for i, (src, dst) in enumerate(pairs)
    ]
    for load in sum(block_loads, []) + loads:
        load.start()

    barrier = pltpu.get_barrier_semaphore()

    def greet(k, carry):
        d = lax.rem(me + k, n)
        pl.semaphore_signal(
            barrier,
            inc=1,
            device_id=(lax.div(d, inner_count), lax.rem(d, inner_count)),
            device_id_type=pl.DeviceIdType.MESH,
        )
        return carry

    lax.fori_loop(1, n, greet, 0)

    def copy_to(src, dst, kind, d):
        return pltpu.make_async_remote_copy(
            src_ref=src,
            dst_ref=dst,
            send_sem=send_sems.at[kind[0], kind[1]],
            recv_sem=recv_sems.at[kind[0], kind[1]],
            device_id=(lax.div(d, inner_count), lax.rem(d, inner_count)),
            device_id_type=pl.DeviceIdType.MESH,
        )

    rest = n - inner_count
    other = lax.rem(me + 1, n)

    def spread(src, dst, c, kind, tensors):
        def cross(k, carry):
            group = ctx_idx + 1 + lax.div(k, inner_count)
            d = lax.rem(group * inner_count + lax.rem(inner_idx + k, inner_count), n)
            copy_to(src.at[c, d, tensors], dst.at[c, me, tensors], (kind + 1, c), d).start()
            return carry

        def own(k, carry):
            d = ctx_idx * inner_count + lax.rem(inner_idx + k, inner_count)
            copy_to(src.at[c, d], dst.at[c, me], (kind, c), d).start()
            return carry

        lax.fori_loop(0, rest, cross, 0)
        lax.fori_loop(1, inner_count, own, 0)

    def spread_all(src, dst, c, kind, tensors):
        few, many = pl.ds(0, inner_count - 1), pl.ds(0, rest)
        return (
            copy_to(src.at[c, few], dst.at[c, few], (kind, c), other),
            copy_to(src.at[c, many, tensors], dst.at[c, many, tensors], (kind + 1, c), other),
        )

    shared, full = pl.ds(0, 2), pl.ds(0, 3)

    def start_in(c):
        spread(send, got, c, 0, shared)

    def all_in(c):
        return spread_all(send, got, c, 0, shared)

    def all_out(c):
        return spread_all(out, back, c, 2, full if c == chunks - 1 else shared)

    def relays(c):
        if c == chunks - 1:
            return []
        group = pl.ds(pl.multiple_of(ctx_idx * inner_count, inner_count), inner_count)
        return [
            copy_to(
                back.at[c, group, 2],
                back.at[c, group, 2],
                (3 + p, c),
                lax.rem(me + p * inner_count, n),
            )
            for p in range(1, ctx_count)
        ]

    def by_channel(block):
        return jnp.transpose(block).reshape(n, SUBLANES, width)

    for c in range(chunks):
        cols = slice(c * span, (c + 1) * span)
        for load in block_loads[c]:
            load.wait()
        send[c, :, 0] = by_channel(value[:, cols])
        send[c, :, 1] = by_channel(cot[:, cols] * gate[:, cols])
        send[c, :, 2] = by_channel(taps[:, cols])
        if c == 0:
            pl.semaphore_wait(barrier, n - 1)
        start_in(c)
        got[c, me] = send[c, me]

    for load in loads:
        load.wait()
    rows = [rate[...], coeff[...], keep[...]]
    filled = sum(r.shape[0] for r in rows)
    rows.append(jnp.zeros((LANES - filled, rate.shape[1]), jnp.float32))
    params[...] = jnp.transpose(jnp.concatenate(rows, 0))
    cosine, sine = circle[:, :width], circle[:, width:]
    for high, low, sign in ((ahead_high, ahead_low, 1.0), (behind_high, behind_low, -1.0)):
        table = jnp.concatenate(
            [
                jnp.concatenate([cosine, -sign * sine], 1),
                jnp.concatenate([sign * sine, cosine], 1),
            ],
            0,
        )
        top = table.astype(jnp.bfloat16)
        high[...] = top
        low[...] = (table - top.astype(jnp.float32)).astype(jnp.bfloat16)
    spec[:, half] = jnp.zeros(spec.shape[:1] + spec.shape[2:], jnp.float32)

    lane = lax.broadcasted_iota(jnp.int32, (SUBLANES, width), 1).astype(jnp.float32)

    def per_channel(chunk):
        own = params[pl.ds(pl.multiple_of(chunk * span + me * SUBLANES, SUBLANES), SUBLANES), :]

        def wide(column):
            return jnp.broadcast_to(own[:, column : column + 1], (SUBLANES, width))

        rates = [wide(m) for m in range(modes)]
        coeffs = [wide(modes + m) for m in range(modes)]
        keeps = [
            [wide((2 + g) * modes + m) for m in range(modes)] for g in range(ctx_count - 1)
        ]
        return rates, coeffs, keeps

    def add_tail(c):
        rates, coeffs, _ = per_channel(c)
        steps = [jnp.exp(-r * float(width)) for r in rates]
        terms = [f * jnp.exp(-r * lane) for r, f in zip(rates, coeffs)]
        base = ctx_idx * inner_count
        for i in range(inner_count):
            got[c, base + i, 2] = got[c, base + i, 2] + sum(terms[1:], terms[0])
            terms = [t * s for t, s in zip(terms, steps)]

    def rows_ahead(c, base, tensor, slot):
        blank = (None, None)
        xs = [(got[c, base + i, tensor], None) for i in range(inner_count)] + [blank] * inner_count
        parts = transform_ahead(xs)
        for k in range(half):
            real, imag = parts[k]
            cosine, sine = twist[0, k : k + 1, :], twist[1, k : k + 1, :]
            if imag is None:
                first, second = real * cosine, -(real * sine)
            else:
                first, second = real * cosine + imag * sine, imag * cosine - real * sine
            spec[slot, k, :, :width] = first
            spec[slot, k, :, width:] = second

    def lines(high, low):
        data = spec[...].reshape(-1, 2 * width)
        top = data.astype(jnp.bfloat16)
        rest_part = (data - top.astype(jnp.float32)).astype(jnp.bfloat16)
        dot = functools.partial(jnp.dot, preferred_element_type=jnp.float32)
        result = dot(rest_part, high[...]) + dot(top, low[...]) + dot(top, high[...])
        spec[...] = result.reshape(spec.shape)

    def rows_behind(slot):
        xs = []
        for k in range(half):
            real, imag = spec[slot, k, :, :width], spec[slot, k, :, width:]
            cosine, sine = twist[2, k : k + 1, :], twist[3, k : k + 1, :]
            xs.append((real * cosine - imag * sine, real * sine + imag * cosine))
        xs += [(None, None)] * (row_count - half)
        return [y[0] for y in transform_behind(xs)[:inner_count]]

    kern_slot, value_slot, grad_slot = 0, 1, 1 + ctx_count
    grad_scale = 1.0 / math.sqrt(group_len * ctx_count)

    def multiply(k, carry):
        def load(slot):
            return spec[slot, k, :, :width], spec[slot, k, :, width:]

        def store(slot, real, imag):
            spec[slot, k, :, :width] = real
            spec[slot, k, :, width:] = imag

        kr, ki = load(kern_slot)
        corr_r = corr_i = 0.0
        for g in range(ctx_count):
            vr, vi = load(value_slot + g)
            gr, gi = load(grad_slot + g)
            corr_r = corr_r + (vr * gr + vi * gi)
            corr_i = corr_i + (vr * gi - vi * gr)
            store(value_slot + g, kr * vr - ki * vi, kr * vi + ki * vr)
            store(grad_slot + g, kr * gr + ki * gi, kr * gi - ki * gr)
        store(kern_slot, corr_r, corr_i)
        return carry

    def carried_ahead(chunk):
        rates, coeffs, keeps = per_channel(chunk)
        steps = [jnp.exp(-r * float(width)) for r in rates]
        whole = [jnp.exp(-r * float(group_len)) for r in rates]
        to_end = [jnp.exp(-r * (width - 1.0 - lane)) for r in rates]
        from_start = [c * jnp.exp(-r * (lane + 1.0)) for r, c in zip(rates, coeffs)]
        state = [jnp.zeros((SUBLANES, 1), jnp.float32)] * modes
        for g in range(ctx_count - 1):
            acc = [jnp.zeros((SUBLANES, width), jnp.float32)] * modes
            for i in range(inner_count):
                block = got[chunk, g * inner_count + i, 0]
                acc = [a * s + block for a, s in zip(acc, steps)]
            for m in range(modes):
                total = jnp.sum(acc[m] * to_end[m], 1, keepdims=True)
                state[m] = keeps[g][m][:, :1] * (whole[m][:, :1] * state[m] + total)
            terms = [f * st for f, st in zip(from_start, state)]
            for i in range(inner_count):
                row = (g + 1) * inner_count + i
                out[chunk, row, 0] = out[chunk, row, 0] + sum(terms[1:], terms[0])
                terms = [t * s for t, s in zip(terms, steps)]

    def carried_behind(chunk):
        rates, coeffs, keeps = per_channel(chunk)
        steps = [jnp.exp(-r * float(width)) for r in rates]
        whole = [jnp.exp(-r * float(group_len)) for r in rates]
        to_end = [jnp.exp(-r * (width - 1.0 - lane)) for r in rates]
        from_start = [c * jnp.exp(-r * (lane + 1.0)) for r, c in zip(rates, coeffs)]
        state = [jnp.zeros((SUBLANES, 1), jnp.float32)] * modes
        for g in reversed(range(1, ctx_count)):
            acc = [jnp.zeros((SUBLANES, width), jnp.float32)] * modes
            for i in reversed(range(inner_count)):
                block = got[chunk, g * inner_count + i, 1]
                acc = [a * s + block for a, s in zip(acc, steps)]
            for m in range(modes):
                total = jnp.sum(acc[m] * from_start[m], 1, keepdims=True)
                if g < ctx_count - 1:
                    state[m] = total + whole[m][:, :1] * keeps[g][m][:, :1] * state[m]
                else:
                    state[m] = total
            terms = [
                t * (kp[:, :1] * st) for t, kp, st in zip(to_end, keeps[g - 1], state)
            ]
            for i in reversed(range(inner_count)):
                row = (g - 1) * inner_count + i
                out[chunk, row, 1] = out[chunk, row, 1] + sum(terms[1:], terms[0])
                terms = [t * s for t, s in zip(terms, steps)]

    def process(c, carry):
        for whole in all_in(c):
            whole.wait_recv()
        add_tail(c)
        rows_ahead(c, ctx_idx * inner_count, 2, kern_slot)

        def ahead(step, inner_carry):
            tensor, g = lax.div(step, ctx_count), lax.rem(step, ctx_count)
            rows_ahead(c, g * inner_count, tensor, 1 + step)
            return inner_carry

        lax.fori_loop(0, 2 * ctx_count, ahead, 0)
        lines(ahead_high, ahead_low)
        lax.fori_loop(0, half, multiply, 0)
        lines(behind_high, behind_low)
        for i, y in enumerate(rows_behind(kern_slot)):
            y = y * grad_scale
            for g in range(ctx_count):
                out[c, g * inner_count + i, 2] = y

        def behind(step, inner_carry):
            tensor, g = lax.div(step, ctx_count), lax.rem(step, ctx_count)
            for i, y in enumerate(rows_behind(1 + step)):
                out[c, g * inner_count + i, tensor] = y
            return inner_carry

        lax.fori_loop(0, 2 * ctx_count, behind, 0)
        carried_ahead(c)
        carried_behind(c)
        back[c, me] = out[c, me]

        @pl.when(c < chunks - 1)
        def _():
            spread(out, back, c, 2, shared)

        @pl.when(c == chunks - 1)
        def _():
            spread(out, back, c, 2, full)

        return carry

    lax.fori_loop(0, chunks, process, 0)

    def by_token(c, tensor):
        return jnp.transpose(back[c, :, tensor].reshape(span, width))

    for c in range(chunks):
        if c < chunks - 1:
            all_out(c)[0].wait_recv()
        for relay in relays(c):
            relay.start()
    stores = []
    for c in range(chunks):
        cols = slice(c * span, (c + 1) * span)
        if c == chunks - 1:
            all_out(c)[0].wait_recv()
        all_out(c)[1].wait_recv()
        mixture = by_token(c, 0)
        mixed_out[:, cols] = gate[:, cols] * mixture
        grad_gate[:, cols] = cot[:, cols] * mixture
        grad_value[:, cols] = by_token(c, 1)
        for relay in relays(c):
            relay.wait_recv()
        grad_filter[:, cols] = by_token(c, 2)
        moves = (
            (mixed_out, mixed_hbm),
            (grad_gate, gated_hbm),
            (grad_value, turned_hbm),
            (grad_filter, filtered_hbm),
        )
        for i, (src, dst) in enumerate(moves):
            part = pl.ds(c * span, span)
            store = pltpu.make_async_copy(src.at[:, part], dst.at[:, part], store_sems.at[i, c])
            store.start()
            stores.append(store)
    for c in range(chunks):
        for whole in (*all_in(c), *all_out(c), *relays(c)):
            whole.wait_send()
    for store in stores:
        store.wait()


def finish_kernel(*refs):
    sources, targets, held, load_sems, store_sems = refs[:4], refs[4:8], refs[8:12], refs[12], refs[13]
    loads = [
        pltpu.make_async_copy(src, mid, load_sems.at[i])
        for i, (src, mid) in enumerate(zip(sources, held))
    ]
    stores = [
        pltpu.make_async_copy(mid, dst, store_sems.at[i])
        for i, (mid, dst) in enumerate(zip(held, targets))
    ]
    for load in loads:
        load.start()
    for load, store in zip(loads, stores):
        load.wait()
        store.start()
    for store in stores:
        store.wait()


def fits(mesh, value_input):
    inner_count, ctx_count = mesh.shape["inner"], mesh.shape["ctx"]
    tok_dev, channels = value_input.shape
    return (
        tok_dev == LANES
        and ctx_count > 1
        and channels % (inner_count * ctx_count * SUBLANES) == 0
        and inner_count & (inner_count - 1) == 0
    )


def shards_by_channel(
    mesh, gate_input, value_input, filter_taps, decay_rate, mode_coeff, boundary_keep, cotangent
):
    inner_count, ctx_count = mesh.shape["inner"], mesh.shape["ctx"]
    n = inner_count * ctx_count
    tok_dev, channels = value_input.shape
    modes = decay_rate.shape[0]
    chunks = channels // (n * SUBLANES)
    half = inner_count + 1
    tables = line_tables(tok_dev, 2 * inner_count, half)
    keep_rows = boundary_keep.reshape(-1, channels)
    block = jax.ShapeDtypeStruct((tok_dev, channels), jnp.float32)
    f32 = functools.partial(pltpu.VMEM, dtype=jnp.float32)
    pieces = f32((chunks, n, 3, SUBLANES, tok_dev))
    hbm = pl.BlockSpec(memory_space=pltpu.HBM)
    operands = (
        gate_input,
        value_input,
        filter_taps,
        decay_rate,
        mode_coeff,
        keep_rows,
        cotangent,
        *tables,
    )
    results = pl.pallas_call(
        functools.partial(mixer_kernel, ctx_count, inner_count, modes),
        out_shape=(block,) * 4,
        in_specs=[hbm] * len(operands),
        out_specs=(hbm,) * 4,
        scratch_shapes=[pltpu.VMEM(a.shape, a.dtype) for a in operands]
        + [pltpu.VMEM((2 * tok_dev, 2 * tok_dev), jnp.bfloat16)] * 4
        + [
            pieces,
            pieces,
            f32((1 + 2 * ctx_count, half + 1, SUBLANES, 2 * tok_dev)),
            f32((channels, LANES)),
            pieces,
            pieces,
        ]
        + [f32((tok_dev, channels))] * 4
        + [
            pltpu.SemaphoreType.DMA((4, chunks)),
            pltpu.SemaphoreType.DMA((len(operands),)),
            pltpu.SemaphoreType.DMA((4, chunks)),
            pltpu.SemaphoreType.DMA((3 + ctx_count, chunks)),
            pltpu.SemaphoreType.DMA((3 + ctx_count, chunks)),
        ],
        compiler_params=pltpu.CompilerParams(
            collective_id=0, has_side_effects=True, vmem_limit_bytes=60 * 1024 * 1024
        ),
    )(*operands)
    return pl.pallas_call(
        finish_kernel,
        out_shape=(block,) * 4,
        in_specs=[hbm] * 4,
        out_specs=(hbm,) * 4,
        scratch_shapes=[f32((tok_dev, channels))] * 4
        + [pltpu.SemaphoreType.DMA((4,)), pltpu.SemaphoreType.DMA((4,))],
        compiler_params=pltpu.CompilerParams(vmem_limit_bytes=60 * 1024 * 1024),
    )(*results)


def shards_of(mesh, *args):
    if fits(mesh, args[1]):
        return shards_by_channel(mesh, *args)
    return shards(*args)


def solution(mesh):
    placed = (
        P(("ctx", "inner"), None),
        P(("ctx", "inner"), None),
        P("inner", None),
        P(),
        P(),
        P(),
        P(("ctx", "inner"), None),
    )
    return jax.shard_map(
        functools.partial(shards_of, mesh),
        mesh=mesh,
        in_specs=placed,
        out_specs=(
            P(("ctx", "inner"), None),
            P(("ctx", "inner"), None),
            P(("ctx", "inner"), None),
            P("inner", None),
        ),
        check_vma=False,
    )
```
